512 devices in a mesh: blk: 32 (over z, core), bond: 16 (over y, x).
Axes of the slice: x: 4, y: 4, z: 16, core: 2. Of those that a mesh axis runs over, the one named last changes fastest.
Arguments:
- iso: bfloat16 [32, 256, 256, 256], P('blk', None, 'bond'), may hold values from -0.03125 to 0.03125
- edge_left: bfloat16 [32, 256, 256], P('blk'), may hold values from -0.375 to 0.375
- edge_right: bfloat16 [32, 256, 256], P('blk'), may hold values from -0.375 to 0.375
- coupling: float32 [32, 256, 256], P('blk'), may hold values from -0.25 to 0.25
Outputs:
- iso_out: bfloat16 [32, 256, 256, 256], P('blk', None, 'bond')
- top_env: float32 [32, 256, 256], P('blk')
The draws below stay inside these ranges and needn't reach their ends.
All inputs are finite; a program needn't handle non-finite values.
Results may differ from the reference program's by a relative error of at most 0.00105.
The reference program's roundings to bfloat16 on the way count: a program that leaves them out, or rounds other values in their place, can miss the bound.
Values may be sent and summed in bfloat16 or wider, within the bound.
No kernel may reach another device: no remote copies, remote signals or barrier semaphores. Data moves between devices by JAX's collectives and lax.ppermute only.
A program may use at most 64 MiB of HBM per device.

```python
import math
import jax
import jax.numpy as jnp
from jax import lax

CHI = 256
NEWTON = 2
SUBTREES = 32
LEVELS = 5
CB = 16


def draw_iso(key, part):
    ranks = 4
    sigma = 1.0 / CHI
    block_ids = jnp.arange(CHI, dtype=jnp.int32) // CB
    block_weights = jax.random.uniform(jax.random.fold_in(key, 7001), (ranks, CHI // CB), jnp.float32, 0.0, 1.0)
    per_column = jnp.take(block_weights, block_ids, axis=1)
    strength = 0.5

    def one_subtree(index):
        subkey = jax.random.fold_in(jax.random.fold_in(key, 7002), index)
        first_key, second_key, third_key = jax.random.split(subkey, 3)
        base = jnp.clip(jax.random.normal(first_key, (CHI, CHI, CHI), jnp.float32), -6.0, 6.0)
        shared = jax.random.normal(second_key, (ranks, CHI, CHI), jnp.float32) * per_column[:, None, :]
        columns = jax.random.normal(third_key, (ranks, CHI), jnp.float32)
        common = jnp.einsum('rab,rp->abp', shared, columns) * (strength / math.sqrt(ranks))
        values = jnp.clip(sigma * (base + common), -8.0 * sigma, 8.0 * sigma)
        return values.astype(jnp.bfloat16)
    return lax.map(one_subtree, jnp.arange(SUBTREES, dtype=jnp.int32))


def block_scale(own_key, extent, cuts, smallest, top_value):
    loudness, own = 1.0, jax.random.fold_in(own_key, 6)
    for position, shards_of in cuts:
        draws = jnp.exp(jax.random.uniform(jax.random.fold_in(own, position), (shards_of,), jnp.float32, smallest / len(cuts), top_value / len(cuts)))
        loudness = loudness * jnp.repeat(draws, extent[position] // shards_of).reshape([-1 if axis == position else 1 for axis in range(len(extent))])
    return loudness


def normal_values(own_key, shape, width, reach, pieces=(), held_as=jnp.bfloat16):
    entries = width * jax.random.normal(own_key, shape, jnp.float32)
    if pieces:
        entries = entries * block_scale(own_key, shape, pieces, -0.22, 0.18)
    return jnp.clip(entries, -reach, reach).astype(held_as)


def setup_inputs(seed: int = 0) -> dict:
    key_of = jax.random.split(jax.random.key(seed), 5)
    iso = draw_iso(jax.random.fold_in(key_of[4], 71), 0)
    edge_left = normal_values(key_of[1], (SUBTREES, CHI, CHI), CHI ** -0.5, 0.375, ((0, 32),))
    edge_right = normal_values(key_of[2], (SUBTREES, CHI, CHI), CHI ** -0.5, 0.375, ((0, 32),))
    coupling = normal_values(key_of[3], (SUBTREES, CHI, CHI), (2 * CHI) ** -0.5, 0.25, ((0, 32),), jnp.float32)
    return {"iso": iso, "edge_left": edge_left, "edge_right": edge_right, "coupling": coupling}


highest = lax.Precision.HIGHEST

def ascend_pair(packed):
    iso_one, left_one, right_one = packed
    wide_iso = iso_one.astype(jnp.float32)
    operators = jnp.stack([left_one, right_one]).astype(jnp.float32)
    mapped = jnp.einsum('kxa,abp->kxbp', operators, wide_iso, precision=highest)
    return jnp.einsum('abp,kabq->kpq', wide_iso, mapped, precision=highest)

def update_one(packed):
    iso_one, mix_one, top_one = packed
    wide_iso = iso_one.astype(jnp.float32)
    gradient = jnp.einsum('xa,abp->xbp', mix_one.astype(jnp.float32), wide_iso, precision=highest)
    gradient = gradient + jnp.einsum('abq,qp->abp', wide_iso, top_one.astype(jnp.float32), precision=highest)
    flattened = gradient.reshape(CHI * CHI, CHI)
    flattened = flattened * lax.rsqrt(jnp.sum(flattened * flattened) + 1e-06)
    for newton_step in range(NEWTON):
        gram_mat = jnp.dot(flattened.T, flattened, precision=highest)
        flattened = 1.5 * flattened - 0.5 * jnp.dot(flattened, gram_mat, precision=highest)
    return flattened.reshape(CHI, CHI, CHI).astype(jnp.bfloat16)

def reference(iso, edge_left, edge_right, coupling):
    ascended = lax.map(ascend_pair, (iso, edge_left, edge_right)).astype(jnp.bfloat16)
    left_bounds = ascended[:, 0]
    right_bounds = ascended[:, 1]
    environ = left_bounds.astype(jnp.float32) + right_bounds.astype(jnp.float32)
    subtree_ids = jnp.arange(SUBTREES, dtype=jnp.int32)
    for level_idx in range(LEVELS):
        partner = environ[jnp.bitwise_xor(subtree_ids, 1 << level_idx)]
        mapped = jnp.einsum('sij,sjk,slk->sil', coupling, partner, coupling, precision=highest)
        environ = 0.5 * (environ + mapped)
    top_low = environ.astype(jnp.bfloat16)
    mixed_op = edge_left.astype(jnp.float32) + jnp.roll(right_bounds, 1, axis=0).astype(jnp.float32)
    mixed_op = (mixed_op + jnp.roll(left_bounds, -1, axis=0).astype(jnp.float32)).astype(jnp.bfloat16)
    iso_out = lax.map(update_one, (iso, mixed_op, top_low))
    return (iso_out, environ)
```

```python
import jax
import jax.numpy as jnp
from jax import lax
from jax.sharding import PartitionSpec as P

bf16 = jnp.bfloat16
f32 = jnp.float32


def split(x):
    rounded = lax.reduce_precision(x, 8, 7)
    return rounded.astype(bf16), (x - rounded).astype(bf16)


def mm(a, b, dims=((1,), (0,))):
    return lax.dot_general(a, b, (dims, ((), ())), preferred_element_type=f32)


def mm3(a, b, dims=((1,), (0,))):
    ah, al = split(a)
    bh, bl = split(b)
    return mm(ah, bh, dims) + (mm(ah, bl, dims) + mm(al, bh, dims))


NT = ((1,), (1,))
TN = ((0,), (0,))


def sandwich(c, e):
    return mm3(mm3(c, e), c, NT)


def exchange(x, axis, groups=None):
    return lax.all_to_all(x, axis, 0, 0, axis_index_groups=groups, tiled=True)


def permuted(x, axis, route):
    return lax.ppermute(x, axis, [(i, route(i)) for i in range(lax.axis_size(axis))])


def body(iso, edge_left, edge_right, coupling):
    iso = iso[0]
    couple = coupling[0]
    size = iso.shape[0]
    width = lax.axis_size("bond")
    rows = size // width
    s = lax.axis_index("blk")
    j = lax.axis_index("bond")
    z = s // 2
    flat = iso.reshape(-1, size)

    couple_1 = permuted(couple, "blk", lambda i: i ^ 2)
    couple_2 = permuted(couple, "blk", lambda i: i ^ 8)

    operators = jnp.concatenate([edge_left[0], edge_right[0]], axis=0)
    mapped = jnp.einsum("xa,abp->xbp", operators, iso, preferred_element_type=f32)
    hi, lo = split(mapped)

    def contract(part):
        part = part.reshape(2, -1, size)
        return jnp.einsum("rp,krq->kpq", flat, part, preferred_element_type=f32)

    partial = contract(hi) + contract(lo)
    blocks = partial.reshape(2, width, rows, size).transpose(1, 0, 2, 3)
    share = exchange(blocks, "bond").sum(axis=0).astype(bf16)
    gathered = exchange(jnp.broadcast_to(share[None], (width, *share.shape)), "bond")
    gathered = gathered.transpose(1, 0, 2, 3).reshape(2, size, size)

    near = permuted(gathered, "blk", lambda i: i ^ 1)
    odd = s % 2 == 1
    outward = jnp.where(odd, gathered[1], gathered[0])
    far = permuted(outward, "blk", lambda i: (i + 1) % 32 if i % 2 else (i - 1) % 32)
    from_left = jnp.where(odd, near[1], far)
    from_right = jnp.where(odd, far, near[0])
    mix = edge_left[0].astype(f32) + from_left.astype(f32) + from_right.astype(f32)
    mix = mix.astype(bf16)

    env = gathered[0].astype(f32) + gathered[1].astype(f32)
    env_near = near[0].astype(f32) + near[1].astype(f32)
    env = 0.5 * (env + sandwich(couple, env_near))

    moved = jnp.einsum("xa,abp->xbp", mix, iso, preferred_element_type=f32).reshape(-1, size)
    moved_hi, moved_lo = split(moved)
    part_q = mm(flat, moved_hi, TN) + mm(flat, moved_lo, TN)
    cross = mm(moved_hi, moved_lo, TN)
    part_r = mm(moved_hi, moved_hi, TN) + cross + cross.T
    part_n = mm(flat, flat, TN)
    row = lax.broadcasted_iota(jnp.int32, (size, size), 0)
    col = lax.broadcasted_iota(jnp.int32, (size, size), 1)
    part_s = jnp.where(row < col, part_n, part_r)
    diag_n = jnp.sum(jnp.where(row == col, part_n, 0.0), axis=0)
    diag_r = jnp.sum(jnp.where(row == col, part_r, 0.0), axis=0)
    nh, nl = split(diag_n)
    _, rl = split(diag_r)
    extra = jnp.concatenate(
        [jnp.stack([nh, nl, rl]), jnp.zeros((rows - 3, size), bf16)], axis=0
    )

    def slices(env, foreign, me):
        own = lax.dynamic_slice_in_dim(env, j * rows, rows, 0)
        left = lax.dynamic_slice_in_dim(foreign, j * rows, rows, 0)
        crossed = mm3(mm3(left, env), foreign, NT)
        which = lax.broadcasted_iota(jnp.int32, (4, 1, 1), 0) ^ me
        return jnp.where(which == 0, 0.0, jnp.where(which == 3, crossed[None], own[None]))

    quads = [[(zq * 4 + zl) * 2 + c for zl in range(4)] for zq in range(4) for c in range(2)]
    strides = [[(zh * 4 + zl) * 2 + c for zh in range(4)] for zl in range(4) for c in range(2)]

    incoming = exchange(slices(env, couple_1, z % 4), "blk", quads).sum(axis=0)
    fh, fl = split(incoming)
    spread = jnp.broadcast_to(
        jnp.stack([fh, fl, extra])[None], (width, 3, rows, size)
    )
    shares = jnp.stack([part_q, part_s]).astype(bf16).reshape(2, width, rows, size).transpose(1, 0, 2, 3)
    got = exchange(jnp.concatenate([spread, shares], axis=1), "bond")
    force = (got[:, 0].astype(f32) + got[:, 1].astype(f32)).reshape(size, size)
    extras = got[:, 2].astype(f32).sum(axis=0)
    sums = got[:, 3:].astype(f32).sum(axis=0).astype(bf16)
    env = 0.25 * (env + sandwich(couple, force))

    incoming = exchange(slices(env, couple_2, z // 4), "blk", strides).sum(axis=0)
    fh, fl = split(incoming)
    spread = jnp.concatenate([jnp.stack([fh, fl]), sums], axis=0)
    got = exchange(jnp.broadcast_to(spread[None], (width, *spread.shape)), "bond")
    got = got.transpose(1, 0, 2, 3).reshape(4, size, size).astype(f32)
    env = 0.25 * (env + sandwich(couple, got[0] + got[1]))

    full_q, full_s = got[2], got[3]
    lower = jnp.where(row > col, full_s, 0.0)
    upper = jnp.where(row < col, full_s, 0.0)
    full_n = upper + upper.T + jnp.where(row == col, (extras[0] + extras[1])[None, :], 0.0)
    full_r = lower + lower.T + jnp.where(row == col, full_s + extras[2][None, :], 0.0)
    top = lax.reduce_precision(env, 8, 7)
    half = full_q + 0.5 * mm3(full_n, top)
    side = mm3(half, top, TN)
    gram = full_r + side + side.T
    trace = jnp.sum(jnp.where(row == col, gram, 0.0))
    factor = lax.rsqrt(trace + 1e-06)
    g = gram * (factor * factor)
    g2 = mm3(g, g)
    eye = jnp.where(row == col, 1.0, 0.0)
    poly = 2.25 * eye - 2.4375 * g + mm3(g2, 1.6875 * eye - 0.5625 * g + 0.0625 * g2)
    poly = poly * factor
    low = mm3(top, poly)
    ph, pl_ = split(poly)
    lh, ll = split(low)
    out = (mm(moved_hi, ph) + mm(flat, lh)) + (mm(moved_lo, ph) + mm(moved_hi, pl_) + mm(flat, ll))
    return (out.reshape(iso.shape).astype(bf16)[None], env[None])


def solution(mesh):
    placed = (
        P("blk", None, "bond", None),
        P("blk", None, None),
        P("blk", None, None),
        P("blk", None, None),
    )
    return jax.shard_map(
        body,
        mesh=mesh,
        in_specs=placed,
        out_specs=(P("blk", None, "bond", None), P("blk", None, None)),
        check_vma=False,
    )
```

```python
import jax
import jax.numpy as jnp
from jax import lax
from jax.experimental import pallas as pl
from jax.experimental.pallas import tpu as pltpu
from jax.sharding import PartitionSpec as P

bf16 = jnp.bfloat16
f32 = jnp.float32
NN = ((1,), (0,))
NT = ((1,), (1,))
SIZE = 256
WIDTH = 16
ROWS = SIZE // WIDTH
FLAT = SIZE * ROWS
HALF = 128


def split(x):
    hi = x.astype(bf16)
    return hi, (x - hi.astype(f32)).astype(bf16)


def mm(a, b, dims=NN):
    return lax.dot_general(a, b, (dims, ((), ())), preferred_element_type=f32)


def mm3(a, b, dims=NN):
    ah, al = split(a)
    bh, bl = split(b)
    return mm(ah, bh, dims) + (mm(ah, bl, dims) + mm(al, bh, dims))


def sandwich(c, e):
    return mm3(mm3(c, e), c, NT)


def iotas():
    shape = (SIZE, SIZE)
    return lax.broadcasted_iota(jnp.int32, shape, 0), lax.broadcasted_iota(jnp.int32, shape, 1)


def call(kernel, name, outs, scratch=(), smem=0, unread=0, ins=0, flops=0, grid=None, in_specs=None, out_specs=None):
    vmem = pl.BlockSpec(memory_space=pltpu.VMEM)
    if in_specs is None:
        in_specs = (
            [pl.BlockSpec(memory_space=pltpu.SMEM)] * smem
            + [vmem] * (ins - smem - unread)
            + [pl.BlockSpec(memory_space=pl.ANY)] * unread
        )
        out_specs = [vmem] * len(outs)
    params = dict(grid=grid) if grid else {}
    return pl.pallas_call(
        kernel,
        name=name,
        out_shape=[jax.ShapeDtypeStruct(*o) for o in outs],
        in_specs=in_specs,
        out_specs=out_specs,
        scratch_shapes=scratch,
        compiler_params=pltpu.CompilerParams(vmem_limit_bytes=48 << 20),
        cost_estimate=pl.CostEstimate(flops=flops, bytes_accessed=4 << 20, transcendentals=0),
        **params,
    )


def spread_rows(iso_ref, wide_ref):
    wide = iso_ref[...].reshape(FLAT, SIZE).astype(f32)
    wide_ref[0] = wide[:, :HALF]
    wide_ref[1] = wide[:, HALF:]


def bond_slice(wide_ref, b):
    rows = pl.ds(b, SIZE, stride=ROWS)
    return jnp.concatenate([wide_ref[h, rows, :].astype(bf16) for h in range(2)], axis=1)


def ascend_kernel(iso_ref, left_ref, right_ref, out_ref, wide_ref, turned_ref, mapped_ref):
    edges = jnp.concatenate([left_ref[...], right_ref[...]], axis=0)
    spread_rows(iso_ref, wide_ref)
    for b in range(ROWS):
        block = bond_slice(wide_ref, b)
        here = slice(b * SIZE, (b + 1) * SIZE)
        turned_ref[:, here] = block.T
        for k, part in enumerate(split(mm(edges, block))):
            mapped_ref[k, here, :SIZE] = part[:SIZE]
            mapped_ref[k, here, SIZE:] = part[SIZE:]
    turned = turned_ref[...]
    total = mm(turned, mapped_ref[0]) + mm(turned, mapped_ref[1])
    for k in range(2):
        out_ref[:, k] = total[:, k * SIZE : (k + 1) * SIZE].reshape(WIDTH, ROWS, SIZE)


def norm_kernel(iso_ref, after_ref, out_ref):
    flat = iso_ref[...].reshape(FLAT, SIZE)
    out_ref[...] = mm(flat.T, flat)


def round_kernel(got_ref, after_ref, out_ref):
    share = got_ref[0]
    for i in range(1, WIDTH):
        share = share + got_ref[i]
    share = share.astype(bf16)
    for i in range(WIDTH):
        out_ref[i] = share


def slices(index_ref, env_ref, foreign_ref, out_ref):
    rows = pl.ds(index_ref[0] * ROWS, ROWS)
    own = env_ref[rows, :]
    crossed = mm3(mm3(foreign_ref[rows, :], env_ref[...]), foreign_ref[...], NT)
    for p in range(4):
        which = index_ref[1] ^ p
        out_ref[p] = jnp.where(which == 3, crossed, jnp.where(which == 0, 0.0, own))


def first_kernel(index_ref, own_ref, near_ref, couple_ref, foreign_ref, after_ref, env_ref, out_ref):
    def whole(ref):
        return (ref[:, 0].astype(f32) + ref[:, 1].astype(f32)).reshape(SIZE, SIZE)

    env_ref[...] = 0.5 * (whole(own_ref) + sandwich(couple_ref[...], whole(near_ref)))
    slices(index_ref, env_ref, foreign_ref, out_ref)


def gradient_kernel(index_ref, iso_ref, edge_ref, near_ref, far_ref, norm_ref, after_ref, hi_ref, lo_ref, out_ref, wide_ref, moved_ref):
    odd = index_ref[2] == 1

    def whole(ref, k):
        return ref[:, k].astype(f32).reshape(SIZE, SIZE)

    from_left = jnp.where(odd, whole(near_ref, 1), whole(far_ref, 1))
    from_right = jnp.where(odd, whole(far_ref, 0), whole(near_ref, 0))
    mix = (edge_ref[...].astype(f32) + from_left + from_right).astype(bf16)
    spread_rows(iso_ref, wide_ref)
    for b in range(ROWS):
        moved = mm(mix, bond_slice(wide_ref, b))
        for h in range(2):
            moved_ref[h, pl.ds(b, SIZE, stride=ROWS), :] = moved[:, h * HALF : (h + 1) * HALF]
    for h in range(2):
        columns = slice(h * HALF, (h + 1) * HALF)
        hi, lo = split(moved_ref[h])
        hi_ref[:, columns] = hi
        lo_ref[:, columns] = lo
    turned = iso_ref[...].reshape(FLAT, SIZE).T
    part_q = mm(turned, hi_ref[...]) + mm(turned, lo_ref[...])
    turned = hi_ref[...].T
    cross = mm(turned, lo_ref[...])
    part_r = mm(turned, hi_ref[...]) + (cross + cross.T)
    part_n = norm_ref[...]
    row, col = iotas()
    diag_n = jnp.sum(jnp.where(row == col, part_n, 0.0), axis=0, keepdims=True)
    diag_r = jnp.sum(jnp.where(row == col, part_r, 0.0), axis=0, keepdims=True)
    nh, nl = split(diag_n)
    _, rl = split(diag_r)
    extra = jnp.concatenate(
        [nh.astype(f32), nl.astype(f32), rl.astype(f32), jnp.zeros((ROWS - 3, SIZE), f32)], axis=0
    ).astype(bf16)
    packed = jnp.where(row < col, part_n, part_r)
    for i in range(WIDTH):
        out_ref[i, :ROWS] = extra
    out_ref[:, ROWS : 2 * ROWS] = part_q.astype(bf16).reshape(WIDTH, ROWS, SIZE)
    out_ref[:, 2 * ROWS :] = packed.astype(bf16).reshape(WIDTH, ROWS, SIZE)


def pack_kernel(got_ref, parts_ref, out_ref):
    hi, lo = split((got_ref[0] + got_ref[1]) + (got_ref[2] + got_ref[3]))
    for i in range(WIDTH):
        out_ref[i, :ROWS] = hi
        out_ref[i, ROWS : 2 * ROWS] = lo
    out_ref[:, 2 * ROWS :] = parts_ref[...]


def repeat_kernel(got_ref, sums_ref, out_ref):
    hi, lo = split((got_ref[0] + got_ref[1]) + (got_ref[2] + got_ref[3]))
    for i in range(WIDTH):
        out_ref[i, :ROWS] = hi
        out_ref[i, ROWS : 2 * ROWS] = lo
        out_ref[i, 2 * ROWS :] = sums_ref[...]


def two_levels(env_ref, got_ref, couple_ref):
    force = got_ref[:, :ROWS].astype(f32) + got_ref[:, ROWS : 2 * ROWS].astype(f32)
    return 0.25 * (env_ref[...] + sandwich(couple_ref[...], force.reshape(SIZE, SIZE)))


def second_kernel(index_ref, got_ref, old_ref, couple_ref, foreign_ref, env_ref, out_ref, sums_ref, extra_ref):
    env_ref[...] = two_levels(old_ref, got_ref, couple_ref)
    slices(index_ref, env_ref, foreign_ref, out_ref)
    total = got_ref[0, 2 * ROWS :].astype(f32)
    for i in range(1, WIDTH):
        total = total + got_ref[i, 2 * ROWS :].astype(f32)
    extra_ref[...] = total[:ROWS]
    sums_ref[...] = total[ROWS:].astype(bf16)


def polar_matrices(env, full_q, full_s, extra_ref):
    row, col = iotas()
    top = env.astype(bf16).astype(f32)
    lower = jnp.where(row > col, full_s, 0.0)
    upper = jnp.where(row < col, full_s, 0.0)
    diag_n = extra_ref[0:1, :] + extra_ref[1:2, :]
    full_n = upper + upper.T + jnp.where(row == col, diag_n, 0.0)
    full_r = lower + lower.T + jnp.where(row == col, full_s + extra_ref[2:3, :], 0.0)
    half = full_q + 0.5 * mm3(full_n, top)
    side = mm3(top.T, half)
    gram = full_r + side + side.T
    trace = jnp.sum(jnp.where(row == col, gram, 0.0), keepdims=True)
    factor = lax.rsqrt(trace + 1e-06)
    g = gram * (factor * factor)
    g2 = mm3(g, g)
    eye = jnp.where(row == col, 1.0, 0.0)
    poly = 2.25 * eye - 2.4375 * g + mm3(g2, 1.6875 * eye - 0.5625 * g + 0.0625 * g2)
    poly = poly * factor
    return poly, mm3(top, poly)


def final_kernel(got_ref, extra_ref, old_ref, couple_ref, iso_ref, hi_ref, lo_ref, env_ref, out_ref, map_ref):
    @pl.when(pl.program_id(0) == 0)
    def _():
        env = two_levels(old_ref, got_ref, couple_ref)
        env_ref[...] = env
        full_q = got_ref[:, 2 * ROWS : 3 * ROWS].astype(f32).reshape(SIZE, SIZE)
        full_s = got_ref[:, 3 * ROWS :].astype(f32).reshape(SIZE, SIZE)
        poly, low = polar_matrices(env, full_q, full_s, extra_ref)
        ph, pl_ = split(poly)
        lh, ll = split(low)
        for k, part in enumerate((ph, ph, pl_, lh, ll)):
            map_ref[k * SIZE : (k + 1) * SIZE] = part

    flat = iso_ref[...].reshape(-1, SIZE)
    hi = hi_ref[...]
    rows = jnp.concatenate([hi, lo_ref[...], hi, flat, flat], axis=1)
    out_ref[...] = mm(rows, map_ref[...]).astype(bf16).reshape(iso_ref.shape)


def exchange(x, axis, groups=None):
    return lax.all_to_all(x, axis, 0, 0, axis_index_groups=groups, tiled=True)


def permuted(x, axis, route):
    return lax.ppermute(x, axis, [(i, route(i)) for i in range(lax.axis_size(axis))])


square = ((SIZE, SIZE), f32)
sliced = ((4, ROWS, SIZE), f32)


def ascend(iso, left, right):
    return call(
        ascend_kernel,
        "ascend",
        [((WIDTH, 2, ROWS, SIZE), f32)],
        scratch=[
            pltpu.VMEM((2, FLAT, HALF), f32),
            pltpu.VMEM((SIZE, FLAT), bf16),
            pltpu.VMEM((2, FLAT, 2 * SIZE), bf16),
        ],
        ins=3,
        flops=6 << 29,
    )(iso, left, right)[0]


def norms(iso, after):
    return call(norm_kernel, "norms", [square], ins=2, unread=1, flops=1 << 29)(iso, after)[0]


def rounded(got, after):
    return call(round_kernel, "rounded", [((WIDTH, 2, ROWS, SIZE), bf16)], ins=2, unread=1)(got, after)[0]


def first(index, own, near, couple, foreign, after):
    return call(first_kernel, "first", [square, sliced], ins=6, smem=1, unread=1)(
        index, own, near, couple, foreign, after
    )


def gradient(index, iso, edge, near, far, norm, after):
    return call(
        gradient_kernel,
        "gradient",
        [((FLAT, SIZE), bf16), ((FLAT, SIZE), bf16), ((WIDTH, 3 * ROWS, SIZE), bf16)],
        scratch=[pltpu.VMEM((2, FLAT, HALF), f32), pltpu.VMEM((2, FLAT, HALF), f32)],
        ins=7,
        smem=1,
        unread=1,
        flops=5 << 29,
    )(index, iso, edge, near, far, norm, after)


def pack(got, parts):
    return call(pack_kernel, "pack", [((WIDTH, 5 * ROWS, SIZE), bf16)], ins=2)(got, parts)[0]


def repeat(got, sums):
    return call(repeat_kernel, "repeat", [((WIDTH, 4 * ROWS, SIZE), bf16)], ins=2)(got, sums)[0]


def second(index, got, old, couple, foreign):
    return call(
        second_kernel,
        "second",
        [square, sliced, ((2 * ROWS, SIZE), bf16), ((ROWS, SIZE), f32)],
        ins=5,
        smem=1,
    )(index, got, old, couple, foreign)


def final(got, extra, old, couple, iso, hi, lo, steps=4):
    vmem = pl.BlockSpec(memory_space=pltpu.VMEM)
    part = pl.BlockSpec((SIZE // steps, ROWS, SIZE), lambda i: (i, 0, 0))
    line = pl.BlockSpec((FLAT // steps, SIZE), lambda i: (i, 0))
    return call(
        final_kernel,
        "final",
        [square, (iso.shape, bf16)],
        scratch=[pltpu.VMEM((5 * SIZE, SIZE), bf16)],
        grid=(steps,),
        in_specs=[vmem] * 4 + [part, line, line],
        out_specs=[vmem, part],
        flops=5 << 29,
    )(got, extra, old, couple, iso, hi, lo)


def body(iso, edge_left, edge_right, coupling):
    iso, left, right, couple = iso[0], edge_left[0], edge_right[0], coupling[0]
    s = lax.axis_index("blk")
    j = lax.axis_index("bond")
    z = s // 2
    index_1 = jnp.stack([j, z % 4, s % 2]).astype(jnp.int32)
    index_2 = jnp.stack([j, z // 4, s % 2]).astype(jnp.int32)

    couple_1 = permuted(couple, "blk", lambda i: i ^ 2)
    couple_2 = permuted(couple, "blk", lambda i: i ^ 8)

    blocks = ascend(iso, left, right)
    norm = norms(iso, blocks)
    share = rounded(exchange(blocks, "bond"), norm)
    own = exchange(share, "bond")
    near = permuted(own, "blk", lambda i: i ^ 1)
    far = permuted(own, "blk", lambda i: (i + 1) % 32 if i % 2 else (i - 1) % 32)

    quads = [[(zq * 4 + zl) * 2 + c for zl in range(4)] for zq in range(4) for c in range(2)]
    strides = [[(zh * 4 + zl) * 2 + c for zh in range(4)] for zl in range(4) for c in range(2)]

    env, outgoing = first(index_1, own, near, couple, couple_1, couple_2)
    incoming = exchange(outgoing, "blk", quads)
    moved_hi, moved_lo, parts = gradient(index_1, iso, left, near, far, norm, outgoing)
    got = exchange(pack(incoming, parts), "bond")
    env, outgoing, sums, extra = second(index_2, got, env, couple, couple_2)
    incoming = exchange(outgoing, "blk", strides)
    got = exchange(repeat(incoming, sums), "bond")
    env, out = final(got, extra, env, couple, iso, moved_hi, moved_lo)
    return (out[None], env[None])


def solution(mesh):
    placed = (
        P("blk", None, "bond", None),
        P("blk", None, None),
        P("blk", None, None),
        P("blk", None, None),
    )
    return jax.shard_map(
        body,
        mesh=mesh,
        in_specs=placed,
        out_specs=(P("blk", None, "bond", None), P("blk", None, None)),
        check_vma=False,
    )
```

```python
import jax
import jax.numpy as jnp
from jax import lax
from jax.experimental import pallas as pl
from jax.experimental.pallas import tpu as pltpu
from jax.sharding import PartitionSpec as P

bf16 = jnp.bfloat16
f32 = jnp.float32
NN = ((1,), (0,))
NT = ((1,), (1,))
SIZE = 256
WIDTH = 16
ROWS = SIZE // WIDTH
FLAT = SIZE * ROWS
HALF = 128
CHUNKS = 4
EXTRA = 8


def split(x):
    hi = x.astype(bf16)
    return hi, (x - hi.astype(f32)).astype(bf16)


def mm(a, b, dims=NN):
    return lax.dot_general(a, b, (dims, ((), ())), preferred_element_type=f32)


def mm3(a, b, dims=NN):
    ah, al = split(a)
    bh, bl = split(b)
    return mm(ah, bh, dims) + (mm(ah, bl, dims) + mm(al, bh, dims))


def sandwich(c, e):
    return mm3(mm3(c, e), c, NT)


def in_hbm(x):
    return pltpu.with_memory_space_constraint(x, pltpu.HBM)


def iotas():
    shape = (SIZE, SIZE)
    return lax.broadcasted_iota(jnp.int32, shape, 0), lax.broadcasted_iota(jnp.int32, shape, 1)


def call(kernel, name, outs, scratch=(), smem=0, unread=0, ins=0, flops=0, grant=16, grid=None, in_specs=None, out_specs=None):
    vmem = pl.BlockSpec(memory_space=pltpu.VMEM)
    if in_specs is None:
        in_specs = (
            [pl.BlockSpec(memory_space=pltpu.SMEM)] * smem
            + [vmem] * (ins - smem - unread)
            + [pl.BlockSpec(memory_space=pl.ANY)] * unread
        )
        out_specs = [vmem] * len(outs)
    params = dict(grid=grid) if grid else {}
    return pl.pallas_call(
        kernel,
        name=name,
        out_shape=[o if isinstance(o, pl.MemoryRef) else jax.ShapeDtypeStruct(*o) for o in outs],
        in_specs=in_specs,
        out_specs=out_specs,
        scratch_shapes=scratch,
        compiler_params=pltpu.CompilerParams(vmem_limit_bytes=grant << 20),
        cost_estimate=pl.CostEstimate(flops=flops, bytes_accessed=4 << 20, transcendentals=0),
        **params,
    )


def spread_rows(iso_ref, wide_ref):
    wide = iso_ref[...].reshape(FLAT, SIZE).astype(f32)
    wide_ref[0] = wide[:, :HALF]
    wide_ref[1] = wide[:, HALF:]


def bond_slice(wide_ref, b):
    rows = pl.ds(b, SIZE, stride=ROWS)
    return jnp.concatenate([wide_ref[h, rows, :].astype(bf16) for h in range(2)], axis=1)


def ascend_kernel(iso_hbm, left_hbm, right_hbm, out_ref, iso_ref, edge_ref, wide_ref, turned_ref, mapped_ref, sems):
    step = SIZE // CHUNKS
    copies = []
    for i in range(CHUNKS):
        here = pl.ds(i * step, step)
        copies.append(pltpu.make_async_copy(iso_hbm.at[here], iso_ref.at[here], sems.at[i]))
    edge_copies = [
        pltpu.make_async_copy(left_hbm, edge_ref.at[pl.ds(0, SIZE)], sems.at[CHUNKS]),
        pltpu.make_async_copy(right_hbm, edge_ref.at[pl.ds(SIZE, SIZE)], sems.at[CHUNKS + 1]),
    ]
    for copy in copies + edge_copies:
        copy.start()
    for i, copy in enumerate(copies):
        copy.wait()
        wide = iso_ref[i * step : (i + 1) * step].reshape(step * ROWS, SIZE).astype(f32)
        for h in range(2):
            wide_ref[h, i * step * ROWS : (i + 1) * step * ROWS] = wide[:, h * HALF : (h + 1) * HALF]
    for copy in edge_copies:
        copy.wait()
    edges = edge_ref[...]
    for b in range(ROWS):
        block = bond_slice(wide_ref, b)
        here = slice(b * SIZE, (b + 1) * SIZE)
        turned_ref[:, here] = block.T
        for k, part in enumerate(split(mm(edges, block))):
            mapped_ref[k, here, :SIZE] = part[:SIZE]
            mapped_ref[k, here, SIZE:] = part[SIZE:]
    turned = turned_ref[...]
    total = mm(turned, mapped_ref[0]) + mm(turned, mapped_ref[1])
    for k in range(2):
        out_ref[:, k] = total[:, k * SIZE : (k + 1) * SIZE].reshape(WIDTH, ROWS, SIZE)


def norm_kernel(iso_ref, after_ref, out_ref):
    flat = iso_ref[...].reshape(FLAT, SIZE)
    out_ref[...] = mm(flat.T, flat)


def round_kernel(got_ref, after_ref, also_ref, out_ref):
    share = got_ref[0]
    for i in range(1, WIDTH):
        share = share + got_ref[i]
    share = share.astype(bf16)
    for i in range(WIDTH):
        out_ref[i] = share


def slices(index_ref, place, env_ref, left, foreign, out_ref):
    own = env_ref[pl.ds(index_ref[0] * ROWS, ROWS), :]
    crossed = mm3(mm3(left, env_ref[...]), foreign, NT)
    for p in range(4):
        which = index_ref[place] ^ p
        out_ref[p] = jnp.where(which == 3, crossed, jnp.where(which == 0, 0.0, own))


def first_kernel(index_ref, own_ref, near_ref, couple_ref, foreign_ref, env_ref, out_ref):
    def whole(ref):
        return (ref[:, 0].astype(f32) + ref[:, 1].astype(f32)).reshape(SIZE, SIZE)

    env_ref[...] = 0.5 * (whole(own_ref) + sandwich(couple_ref[...], whole(near_ref)))
    left = foreign_ref[pl.ds(index_ref[0] * ROWS, ROWS), :]
    slices(index_ref, 1, env_ref, left, foreign_ref[...], out_ref)


def gradient_kernel(index_ref, iso_ref, edge_ref, near_ref, far_ref, norm_ref, after_ref, hi_hbm, lo_hbm, out_ref, wide_ref, moved_ref, hi_ref, lo_ref, sems):
    odd = index_ref[2] == 1

    def whole(ref, k):
        return ref[:, k].astype(f32).reshape(SIZE, SIZE)

    from_left = jnp.where(odd, whole(near_ref, 1), whole(far_ref, 1))
    from_right = jnp.where(odd, whole(far_ref, 0), whole(near_ref, 0))
    mix = (edge_ref[...].astype(f32) + from_left + from_right).astype(bf16)
    spread_rows(iso_ref, wide_ref)
    for b in range(ROWS):
        moved = mm(mix, bond_slice(wide_ref, b))
        for h in range(2):
            moved_ref[h, pl.ds(b, SIZE, stride=ROWS), :] = moved[:, h * HALF : (h + 1) * HALF]
    squares = []
    for h in range(2):
        columns = slice(h * HALF, (h + 1) * HALF)
        moved = moved_ref[h]
        squares.append(jnp.sum(moved * moved, axis=0, keepdims=True))
        hi, lo = split(moved)
        hi_ref[:, columns] = hi
        lo_ref[:, columns] = lo
    copies = [
        pltpu.make_async_copy(hi_ref, hi_hbm, sems.at[0]),
        pltpu.make_async_copy(lo_ref, lo_hbm, sems.at[1]),
    ]
    for copy in copies:
        copy.start()
    turned = iso_ref[...].reshape(FLAT, SIZE).T
    part_q = mm(turned, hi_ref[...])
    part_r = mm(hi_ref[...].T, hi_ref[...])
    part_n = norm_ref[...]
    row, col = iotas()
    diag_n = jnp.sum(jnp.where(row == col, part_n, 0.0), axis=0, keepdims=True)
    diag_r = jnp.concatenate(squares, axis=1)
    part_r = jnp.where(row == col, diag_r, part_r)
    nh, nl = split(diag_n)
    _, rl = split(diag_r)
    extra = jnp.concatenate(
        [nh.astype(f32), nl.astype(f32), rl.astype(f32), jnp.zeros((EXTRA - 3, SIZE), f32)], axis=0
    ).astype(bf16)
    packed = jnp.where(row < col, part_n, part_r)
    out_ref[:, :ROWS] = part_q.astype(bf16).reshape(WIDTH, ROWS, SIZE)
    out_ref[:, ROWS : 2 * ROWS] = packed.astype(bf16).reshape(WIDTH, ROWS, SIZE)
    for i in range(WIDTH):
        out_ref[i, 2 * ROWS :] = extra
    for copy in copies:
        copy.wait()


def pack_kernel(got_ref, parts_ref, foreign_ref, out_ref):
    hi, lo = split((got_ref[0] + got_ref[1]) + (got_ref[2] + got_ref[3]))
    foreign_hi, foreign_lo = split(foreign_ref[...])
    for i in range(WIDTH):
        out_ref[i, :ROWS] = hi
        out_ref[i, ROWS : 2 * ROWS] = lo
        out_ref[i, 4 * ROWS : 5 * ROWS] = foreign_hi
        out_ref[i, 5 * ROWS : 6 * ROWS] = foreign_lo
    out_ref[:, 2 * ROWS : 4 * ROWS] = parts_ref[:, : 2 * ROWS]
    out_ref[:, 6 * ROWS :] = parts_ref[:, 2 * ROWS :]


def repeat_kernel(got_ref, sums_ref, out_ref):
    hi, lo = split((got_ref[0] + got_ref[1]) + (got_ref[2] + got_ref[3]))
    for i in range(WIDTH):
        out_ref[i, :ROWS] = hi
        out_ref[i, ROWS : 2 * ROWS] = lo
        out_ref[i, 2 * ROWS :] = sums_ref[...]


def two_levels(env_ref, got_ref, couple_ref):
    force = got_ref[:, :ROWS].astype(f32) + got_ref[:, ROWS : 2 * ROWS].astype(f32)
    return 0.25 * (env_ref[...] + sandwich(couple_ref[...], force.reshape(SIZE, SIZE)))


def second_kernel(index_ref, got_ref, old_ref, couple_ref, env_ref, out_ref, sums_ref, extra_ref):
    env_ref[...] = two_levels(old_ref, got_ref, couple_ref)

    def foreign(at):
        hi, lo = slice(4 * ROWS, 5 * ROWS), slice(5 * ROWS, 6 * ROWS)
        return got_ref[at, hi].astype(f32) + got_ref[at, lo].astype(f32)

    left = foreign(index_ref[0])
    slices(index_ref, 3, env_ref, left, foreign(slice(None)).reshape(SIZE, SIZE), out_ref)

    def total(rows):
        value = got_ref[0, rows].astype(f32)
        for i in range(1, WIDTH):
            value = value + got_ref[i, rows].astype(f32)
        return value

    extra_ref[...] = total(slice(6 * ROWS, 6 * ROWS + EXTRA))
    sums_ref[...] = total(slice(2 * ROWS, 4 * ROWS)).astype(bf16)


def polar_matrices(env, full_q, full_s, extra_ref):
    row, col = iotas()
    top = env.astype(bf16).astype(f32)
    lower = jnp.where(row > col, full_s, 0.0)
    upper = jnp.where(row < col, full_s, 0.0)
    diag_n = extra_ref[0:1, :] + extra_ref[1:2, :]
    full_n = upper + upper.T + jnp.where(row == col, diag_n, 0.0)
    full_r = lower + lower.T + jnp.where(row == col, full_s + extra_ref[2:3, :], 0.0)
    half = full_q + 0.5 * mm3(full_n, top)
    side = mm3(top.T, half)
    gram = full_r + side + side.T
    trace = jnp.sum(jnp.where(row == col, gram, 0.0), keepdims=True)
    factor = lax.rsqrt(trace + 1e-06)
    g = gram * (factor * factor)
    g2 = mm3(g, g)
    eye = jnp.where(row == col, 1.0, 0.0)
    poly = 2.25 * eye - 2.4375 * g + mm3(g2, 1.6875 * eye - 0.5625 * g + 0.0625 * g2)
    poly = poly * factor
    return poly, mm3(top, poly)


def final_kernel(got_ref, extra_ref, old_ref, couple_ref, iso_ref, hi_ref, lo_ref, env_ref, out_ref, map_ref):
    @pl.when(pl.program_id(0) == 0)
    def _():
        env = two_levels(old_ref, got_ref, couple_ref)
        env_ref[...] = env
        full_q = got_ref[:, 2 * ROWS : 3 * ROWS].astype(f32).reshape(SIZE, SIZE)
        full_s = got_ref[:, 3 * ROWS :].astype(f32).reshape(SIZE, SIZE)
        poly, low = polar_matrices(env, full_q, full_s, extra_ref)
        ph, pl_ = split(poly)
        lh, ll = split(low)
        for k, part in enumerate((ph, ph, pl_, lh, ll)):
            map_ref[k * SIZE : (k + 1) * SIZE] = part

    step = out_ref.shape[0]
    here = pl.program_id(0) * step
    flat = iso_ref[pl.ds(here, step)].reshape(-1, SIZE)
    hi = hi_ref[...]
    rows = jnp.concatenate([hi, lo_ref[...], hi, flat, flat], axis=1)
    out_ref[...] = mm(rows, map_ref[...]).astype(bf16).reshape(out_ref.shape)


def exchange(x, axis, groups=None):
    return lax.all_to_all(x, axis, 0, 0, axis_index_groups=groups, tiled=True)


def permuted(x, axis, route):
    return lax.ppermute(x, axis, [(i, route(i)) for i in range(lax.axis_size(axis))])


square = ((SIZE, SIZE), f32)
kept = pltpu.HBM((SIZE, SIZE), f32)
sliced = ((4, ROWS, SIZE), f32)


def ascend(iso, left, right):
    return call(
        ascend_kernel,
        "ascend",
        [((WIDTH, 2, ROWS, SIZE), f32)],
        scratch=[
            pltpu.VMEM((SIZE, ROWS, SIZE), bf16),
            pltpu.VMEM((2 * SIZE, SIZE), bf16),
            pltpu.VMEM((2, FLAT, HALF), f32),
            pltpu.VMEM((SIZE, FLAT), bf16),
            pltpu.VMEM((2, FLAT, 2 * SIZE), bf16),
            pltpu.SemaphoreType.DMA((CHUNKS + 2,)),
        ],
        in_specs=[pl.BlockSpec(memory_space=pl.ANY)] * 3,
        out_specs=[pl.BlockSpec(memory_space=pltpu.VMEM)],
        grant=24,
        flops=6 << 29,
    )(in_hbm(iso), in_hbm(left), in_hbm(right))[0]


def norms(iso, after):
    return call(norm_kernel, "norms", [square], ins=2, unread=1, flops=1 << 29)(iso, after)[0]


def rounded(got, *after):
    return call(round_kernel, "rounded", [((WIDTH, 2, ROWS, SIZE), bf16)], ins=3, unread=2)(got, *after)[0]


def first(index, own, near, couple, foreign):
    return call(first_kernel, "first", [kept, sliced], ins=5, smem=1)(
        index, own, near, couple, foreign
    )


def gradient(index, iso, edge, near, far, norm, after):
    return call(
        gradient_kernel,
        "gradient",
        [pltpu.HBM((FLAT, SIZE), bf16), pltpu.HBM((FLAT, SIZE), bf16), ((WIDTH, 2 * ROWS + EXTRA, SIZE), bf16)],
        scratch=[
            pltpu.VMEM((2, FLAT, HALF), f32),
            pltpu.VMEM((2, FLAT, HALF), f32),
            pltpu.VMEM((FLAT, SIZE), bf16),
            pltpu.VMEM((FLAT, SIZE), bf16),
            pltpu.SemaphoreType.DMA((2,)),
        ],
        in_specs=[pl.BlockSpec(memory_space=pltpu.SMEM)] + [pl.BlockSpec(memory_space=pltpu.VMEM)] * 5 + [pl.BlockSpec(memory_space=pl.ANY)],
        out_specs=[pl.BlockSpec(memory_space=pl.ANY)] * 2 + [pl.BlockSpec(memory_space=pltpu.VMEM)],
        ins=7,
        smem=1,
        unread=1,
        flops=3 << 29,
        grant=28,
    )(index, iso, in_hbm(edge), in_hbm(near), in_hbm(far), norm, after)


def pack(got, parts, foreign):
    return call(pack_kernel, "pack", [((WIDTH, 6 * ROWS + EXTRA, SIZE), bf16)], ins=3)(got, parts, foreign)[0]


def repeat(got, sums):
    return call(repeat_kernel, "repeat", [((WIDTH, 4 * ROWS, SIZE), bf16)], ins=2)(got, sums)[0]


def second(index, got, old, couple):
    return call(
        second_kernel,
        "second",
        [kept, sliced, ((2 * ROWS, SIZE), bf16), ((EXTRA, SIZE), f32)],
        ins=4,
        smem=1,
    )(index, got, in_hbm(old), couple)


def final(got, extra, old, couple, iso, hi, lo, steps=4):
    vmem = pl.BlockSpec(memory_space=pltpu.VMEM)
    part = pl.BlockSpec((SIZE // steps, ROWS, SIZE), lambda i: (i, 0, 0))
    line = pl.BlockSpec((FLAT // steps, SIZE), lambda i: (i, 0))
    return call(
        final_kernel,
        "final",
        [square, (iso.shape, bf16)],
        scratch=[pltpu.VMEM((5 * SIZE, SIZE), bf16)],
        grid=(steps,),
        in_specs=[vmem] * 5 + [line] * 2,
        out_specs=[vmem, part],
        flops=5 << 29,
    )(got, extra, in_hbm(old), couple, iso, in_hbm(hi), in_hbm(lo))


def body(iso, edge_left, edge_right, coupling):
    iso, left, right, couple = iso[0], edge_left[0], edge_right[0], coupling[0]
    s = lax.axis_index("blk")
    j = lax.axis_index("bond")
    z = s // 2
    index = jnp.stack([j, z % 4, s % 2, z // 4]).astype(jnp.int32)

    couple_1 = permuted(couple, "blk", lambda i: i ^ 2)
    part_2 = lax.dynamic_slice_in_dim(couple, j * ROWS, ROWS, 0)
    part_2 = permuted(part_2, "blk", lambda i: i ^ 8)

    blocks = ascend(iso, left, right)
    norm = norms(iso, blocks)
    share = rounded(exchange(blocks, "bond"), norm, part_2)
    own = exchange(share, "bond")
    near = permuted(own, "blk", lambda i: i ^ 1)
    far = permuted(own, "blk", lambda i: (i + 1) % 32 if i % 2 else (i - 1) % 32)

    quads = [[(zq * 4 + zl) * 2 + c for zl in range(4)] for zq in range(4) for c in range(2)]
    strides = [[(zh * 4 + zl) * 2 + c for zh in range(4)] for zl in range(4) for c in range(2)]

    env, outgoing = first(index, own, near, couple, couple_1)
    incoming = exchange(outgoing, "blk", quads)
    moved_hi, moved_lo, parts = gradient(index, iso, left, near, far, norm, outgoing)
    got = exchange(pack(incoming, parts, part_2), "bond")
    env, outgoing, sums, extra = second(index, got, env, couple)
    incoming = exchange(outgoing, "blk", strides)
    got = exchange(repeat(incoming, sums), "bond")
    env, out = final(got, extra, env, couple, iso, moved_hi, moved_lo)
    return (out[None], env[None])


def solution(mesh):
    placed = (
        P("blk", None, "bond", None),
        P("blk", None, None),
        P("blk", None, None),
        P("blk", None, None),
    )
    return jax.shard_map(
        body,
        mesh=mesh,
        in_specs=placed,
        out_specs=(P("blk", None, "bond", None), P("blk", None, None)),
        check_vma=False,
    )
```

```python
import jax
import jax.numpy as jnp
from jax import lax
from jax.experimental import pallas as pl
from jax.experimental.pallas import tpu as pltpu
from jax.sharding import PartitionSpec as P

bf16 = jnp.bfloat16
f32 = jnp.float32
NN = ((1,), (0,))
NT = ((1,), (1,))
SIZE = 256
WIDTH = 16
ROWS = SIZE // WIDTH
FLAT = SIZE * ROWS
HALF = 128
CHUNKS = 4
EXTRA = 8
PARTS = 8


def split(x):
    hi = x.astype(bf16)
    return hi, (x - hi.astype(f32)).astype(bf16)


def mm(a, b, dims=NN):
    return lax.dot_general(a, b, (dims, ((), ())), preferred_element_type=f32)


def mm3(a, b, dims=NN):
    ah, al = split(a)
    bh, bl = split(b)
    return mm(ah, bh, dims) + (mm(ah, bl, dims) + mm(al, bh, dims))


def sandwich(c, e):
    return mm3(mm3(c, e), c, NT)


def in_hbm(x):
    return pltpu.with_memory_space_constraint(x, pltpu.HBM)


def iotas():
    shape = (SIZE, SIZE)
    return lax.broadcasted_iota(jnp.int32, shape, 0), lax.broadcasted_iota(jnp.int32, shape, 1)


def call(kernel, name, outs, scratch=(), smem=0, unread=0, ins=0, flops=0, grant=16, grid=None, in_specs=None, out_specs=None):
    vmem = pl.BlockSpec(memory_space=pltpu.VMEM)
    any_place = pl.BlockSpec(memory_space=pl.ANY)
    if in_specs is None:
        in_specs = (
            [pl.BlockSpec(memory_space=pltpu.SMEM)] * smem
            + [vmem] * (ins - smem - unread)
            + [any_place] * unread
        )
        out_specs = [any_place if isinstance(o, pl.MemoryRef) else vmem for o in outs]
    params = dict(grid=grid) if grid else {}
    return pl.pallas_call(
        kernel,
        name=name,
        out_shape=[o if isinstance(o, pl.MemoryRef) else jax.ShapeDtypeStruct(*o) for o in outs],
        in_specs=in_specs,
        out_specs=out_specs,
        scratch_shapes=scratch,
        compiler_params=pltpu.CompilerParams(vmem_limit_bytes=grant << 20),
        cost_estimate=pl.CostEstimate(flops=flops, bytes_accessed=4 << 20, transcendentals=0),
        **params,
    )


def spread_rows(iso_ref, wide_ref):
    wide = iso_ref[...].reshape(FLAT, SIZE).astype(f32)
    wide_ref[0] = wide[:, :HALF]
    wide_ref[1] = wide[:, HALF:]


def bond_slice(wide_ref, b):
    rows = pl.ds(b, SIZE, stride=ROWS)
    return jnp.concatenate([wide_ref[h, rows, :].astype(bf16) for h in range(2)], axis=1)


def ascend_kernel(iso_hbm, left_hbm, right_hbm, out_ref, iso_ref, edge_ref, wide_ref, turned_ref, mapped_ref, sems):
    step = SIZE // CHUNKS
    copies = []
    for i in range(CHUNKS):
        here = pl.ds(i * step, step)
        copies.append(pltpu.make_async_copy(iso_hbm.at[here], iso_ref.at[here], sems.at[i]))
    edge_copies = [
        pltpu.make_async_copy(left_hbm, edge_ref.at[pl.ds(0, SIZE)], sems.at[CHUNKS]),
        pltpu.make_async_copy(right_hbm, edge_ref.at[pl.ds(SIZE, SIZE)], sems.at[CHUNKS + 1]),
    ]
    for copy in copies + edge_copies:
        copy.start()
    for i, copy in enumerate(copies):
        copy.wait()
        wide = iso_ref[i * step : (i + 1) * step].reshape(step * ROWS, SIZE).astype(f32)
        for h in range(2):
            wide_ref[h, i * step * ROWS : (i + 1) * step * ROWS] = wide[:, h * HALF : (h + 1) * HALF]
    for copy in edge_copies:
        copy.wait()
    edges = edge_ref[...]
    for b in range(ROWS):
        block = bond_slice(wide_ref, b)
        here = slice(b * SIZE, (b + 1) * SIZE)
        turned_ref[:, here] = block.T
        for k, part in enumerate(split(mm(edges, block))):
            mapped_ref[k, here, :SIZE] = part[:SIZE]
            mapped_ref[k, here, SIZE:] = part[SIZE:]
    turned = turned_ref[...]
    total = mm(turned, mapped_ref[0]) + mm(turned, mapped_ref[1])
    for k in range(2):
        out_ref[:, k] = total[:, k * SIZE : (k + 1) * SIZE].reshape(WIDTH, ROWS, SIZE)


def prepare_kernel(iso_ref, after_ref, block_hbm, turned_hbm, norm_ref, wide_ref, block_ref, turned_ref, sems):
    spread_rows(iso_ref, wide_ref)
    for b in range(ROWS):
        block = bond_slice(wide_ref, b)
        here = slice(b * SIZE, (b + 1) * SIZE)
        block_ref[here] = block
        turned_ref[:, here] = block.T
    copies = [
        pltpu.make_async_copy(block_ref, block_hbm, sems.at[0]),
        pltpu.make_async_copy(turned_ref, turned_hbm, sems.at[1]),
    ]
    for copy in copies:
        copy.start()
    norm_ref[...] = mm(turned_ref[...], block_ref[...])
    for copy in copies:
        copy.wait()


def round_kernel(got_ref, after_ref, also_ref, out_ref):
    share = got_ref[0]
    for i in range(1, WIDTH):
        share = share + got_ref[i]
    share = share.astype(bf16)
    for i in range(WIDTH):
        out_ref[i] = share


def slices(index_ref, place, env_ref, left, foreign, out_ref):
    own = env_ref[pl.ds(index_ref[0] * ROWS, ROWS), :]
    crossed = mm3(mm3(left, env_ref[...]), foreign, NT)
    for p in range(4):
        which = index_ref[place] ^ p
        out_ref[p] = jnp.where(which == 3, crossed, jnp.where(which == 0, 0.0, own))


def first_kernel(index_ref, own_ref, near_ref, couple_ref, foreign_ref, env_hbm, out_ref, env_ref, sem):
    def whole(ref):
        return (ref[:, 0].astype(f32) + ref[:, 1].astype(f32)).reshape(SIZE, SIZE)

    env_ref[...] = 0.5 * (whole(own_ref) + sandwich(couple_ref[...], whole(near_ref)))
    copy = pltpu.make_async_copy(env_ref, env_hbm, sem)
    copy.start()
    left = foreign_ref[pl.ds(index_ref[0] * ROWS, ROWS), :]
    slices(index_ref, 1, env_ref, left, foreign_ref[...], out_ref)
    copy.wait()


def gradient_kernel(index_ref, edge_ref, near_ref, far_ref, norm_ref, block_hbm, turned_hbm, after_ref, mix_ref, out_ref, moved_ref, flipped_ref, block_ref, turned_ref, sems):
    copies = []
    step = FLAT // CHUNKS
    for i in range(CHUNKS):
        here = pl.ds(i * step, step)
        copies.append(pltpu.make_async_copy(block_hbm.at[here], block_ref.at[here], sems.at[2 * i]))
        copies.append(pltpu.make_async_copy(turned_hbm.at[:, here], turned_ref.at[:, here], sems.at[2 * i + 1]))
    for copy in copies:
        copy.start()
    odd = index_ref[2] == 1

    def whole(ref, k):
        return ref[:, k].astype(f32).reshape(SIZE, SIZE)

    from_left = jnp.where(odd, whole(near_ref, 1), whole(far_ref, 1))
    from_right = jnp.where(odd, whole(far_ref, 0), whole(near_ref, 0))
    mix = (edge_ref[...].astype(f32) + from_left + from_right).astype(bf16)
    mix_ref[...] = mix
    squares = jnp.zeros((8, SIZE), f32)
    for b in range(ROWS):
        if b % (ROWS // CHUNKS) == 0:
            at = 2 * b // (ROWS // CHUNKS)
            copies[at].wait()
            copies[at + 1].wait()
        here = slice(b * SIZE, (b + 1) * SIZE)
        moved = mm(mix, block_ref[here])
        squares = squares + jnp.sum((moved * moved).reshape(SIZE // 8, 8, SIZE), axis=0)
        moved_ref[here] = moved.astype(bf16)
        flipped_ref[:, here] = mm(turned_ref[:, here], mix, NT).astype(bf16)
    part_q = mm(turned_ref[...], moved_ref[...])
    part_r = mm(flipped_ref[...], moved_ref[...])
    part_n = norm_ref[...]
    row, col = iotas()
    diag_n = jnp.sum(jnp.where(row == col, part_n, 0.0), axis=0, keepdims=True)
    diag_r = jnp.sum(squares, axis=0, keepdims=True)
    part_r = jnp.where(row == col, diag_r, part_r)
    nh, nl = split(diag_n)
    _, rl = split(diag_r)
    extra = jnp.concatenate(
        [nh.astype(f32), nl.astype(f32), rl.astype(f32), jnp.zeros((EXTRA - 3, SIZE), f32)], axis=0
    ).astype(bf16)
    packed = jnp.where(row < col, part_n, part_r)
    out_ref[:, :ROWS] = part_q.astype(bf16).reshape(WIDTH, ROWS, SIZE)
    out_ref[:, ROWS : 2 * ROWS] = packed.astype(bf16).reshape(WIDTH, ROWS, SIZE)
    for i in range(WIDTH):
        out_ref[i, 2 * ROWS :] = extra


def lines_kernel(mix_ref, block_ref, after_ref, hi_hbm, lo_hbm, moved_ref, hi_ref, lo_ref, sems):
    mix = mix_ref[...]
    for b in range(ROWS):
        moved = mm(mix, block_ref[b * SIZE : (b + 1) * SIZE])
        for h in range(2):
            moved_ref[h, pl.ds(b, SIZE, stride=ROWS), :] = moved[:, h * HALF : (h + 1) * HALF]
    for h in range(2):
        columns = slice(h * HALF, (h + 1) * HALF)
        hi, lo = split(moved_ref[h])
        hi_ref[:, columns] = hi
        lo_ref[:, columns] = lo
    copies = [
        pltpu.make_async_copy(hi_ref, hi_hbm, sems.at[0]),
        pltpu.make_async_copy(lo_ref, lo_hbm, sems.at[1]),
    ]
    for copy in copies:
        copy.start()
    for copy in copies:
        copy.wait()


def pack_kernel(got_ref, parts_ref, foreign_ref, out_ref):
    hi, lo = split((got_ref[0] + got_ref[1]) + (got_ref[2] + got_ref[3]))
    foreign_hi, foreign_lo = split(foreign_ref[...])
    for i in range(WIDTH):
        out_ref[i, :ROWS] = hi
        out_ref[i, ROWS : 2 * ROWS] = lo
        out_ref[i, 4 * ROWS : 5 * ROWS] = foreign_hi
        out_ref[i, 5 * ROWS : 6 * ROWS] = foreign_lo
    out_ref[:, 2 * ROWS : 4 * ROWS] = parts_ref[:, : 2 * ROWS]
    out_ref[:, 6 * ROWS :] = parts_ref[:, 2 * ROWS :]


def repeat_kernel(got_ref, sums_ref, after_ref, out_ref):
    hi, lo = split((got_ref[0] + got_ref[1]) + (got_ref[2] + got_ref[3]))
    for i in range(WIDTH):
        out_ref[i, :ROWS] = hi
        out_ref[i, ROWS : 2 * ROWS] = lo
        out_ref[i, 2 * ROWS :] = sums_ref[...]


def two_levels(env_ref, got_ref, couple_ref):
    force = got_ref[:, :ROWS].astype(f32) + got_ref[:, ROWS : 2 * ROWS].astype(f32)
    return 0.25 * (env_ref[...] + sandwich(couple_ref[...], force.reshape(SIZE, SIZE)))


def second_kernel(index_ref, got_ref, old_ref, couple_ref, env_hbm, out_ref, sums_ref, extra_ref, env_ref, sem):
    env_ref[...] = two_levels(old_ref, got_ref, couple_ref)
    copy = pltpu.make_async_copy(env_ref, env_hbm, sem)
    copy.start()

    def foreign(at):
        hi, lo = slice(4 * ROWS, 5 * ROWS), slice(5 * ROWS, 6 * ROWS)
        return got_ref[at, hi].astype(f32) + got_ref[at, lo].astype(f32)

    left = foreign(index_ref[0])
    slices(index_ref, 3, env_ref, left, foreign(slice(None)).reshape(SIZE, SIZE), out_ref)

    def total(rows):
        value = got_ref[0, rows].astype(f32)
        for i in range(1, WIDTH):
            value = value + got_ref[i, rows].astype(f32)
        return value

    extra_ref[...] = total(slice(6 * ROWS, 6 * ROWS + EXTRA))
    sums_ref[...] = total(slice(2 * ROWS, 4 * ROWS)).astype(bf16)
    copy.wait()


def mm2(a, b, dims=NN):
    ah, al = split(a)
    return mm(ah, b, dims) + mm(al, b, dims)


def polar_matrices(env, full_q, full_s, extra_ref):
    row, col = iotas()
    on = row == col
    top = env.astype(bf16)
    lower = jnp.where(row > col, full_s, 0.0)
    upper = jnp.where(row < col, full_s, 0.0)
    full_n = upper + upper.T + jnp.where(on, extra_ref[0:1, :] + extra_ref[1:2, :], 0.0)
    full_r = lower + lower.T + jnp.where(on, full_s + extra_ref[2:3, :], 0.0)
    half = full_q + 0.5 * mm2(full_n, top)
    hh, hl = split(half)
    turned = top.T
    side = mm(turned, hh) + mm(turned, hl)
    gram = full_r + side + side.T
    trace = jnp.sum(jnp.where(on, gram, 0.0), keepdims=True)
    factor = lax.rsqrt(trace + 1e-06)
    g = gram * (factor * factor)
    g2 = mm3(g, g)
    eye = jnp.where(on, 1.0, 0.0)
    poly = 2.25 * eye - 2.4375 * g + mm3(g2, 1.6875 * eye - 0.5625 * g + 0.0625 * g2)
    poly = poly * factor
    ph, pl_ = split(poly)
    return ph, pl_, mm(top, ph) + mm(top, pl_)


def final_kernel(got_ref, extra_ref, old_ref, couple_ref, iso_ref, hi_hbm, lo_hbm, env_hbm, out_hbm, map_ref, hi_ref, lo_ref, env_ref, out_ref, sems):
    incoming = [
        pltpu.make_async_copy(hi_hbm, hi_ref, sems.at[0]),
        pltpu.make_async_copy(lo_hbm, lo_ref, sems.at[1]),
    ]
    for copy in incoming:
        copy.start()
    env = two_levels(old_ref, got_ref, couple_ref)
    env_ref[...] = env
    outgoing = [pltpu.make_async_copy(env_ref, env_hbm, sems.at[2])]
    outgoing[0].start()
    full_q = got_ref[:, 2 * ROWS : 3 * ROWS].astype(f32).reshape(SIZE, SIZE)
    full_s = got_ref[:, 3 * ROWS :].astype(f32).reshape(SIZE, SIZE)
    ph, pl_, low = polar_matrices(env, full_q, full_s, extra_ref)
    for k, part in enumerate((ph, ph, pl_, *split(low))):
        map_ref[k * SIZE : (k + 1) * SIZE] = part
    for copy in incoming:
        copy.wait()
    step = SIZE // PARTS
    for i in range(PARTS):
        here = pl.ds(i * step, step)
        lines = pl.ds(i * step * ROWS, step * ROWS)
        flat = iso_ref[here].reshape(-1, SIZE)
        hi = hi_ref[lines]
        rows = jnp.concatenate([hi, lo_ref[lines], hi, flat, flat], axis=1)
        out_ref[here] = mm(rows, map_ref[...]).astype(bf16).reshape(step, ROWS, SIZE)
        copy = pltpu.make_async_copy(out_ref.at[here], out_hbm.at[here], sems.at[3 + i])
        copy.start()
        outgoing.append(copy)
    for copy in outgoing:
        copy.wait()


def exchange(x, axis, groups=None):
    return lax.all_to_all(x, axis, 0, 0, axis_index_groups=groups, tiled=True)


def permuted(x, axis, route):
    return lax.ppermute(x, axis, [(i, route(i)) for i in range(lax.axis_size(axis))])


square = ((SIZE, SIZE), f32)
kept = pltpu.HBM((SIZE, SIZE), f32)
held = [pltpu.VMEM((SIZE, SIZE), f32), pltpu.SemaphoreType.DMA]
sliced = ((4, ROWS, SIZE), f32)


def ascend(iso, left, right):
    return call(
        ascend_kernel,
        "ascend",
        [((WIDTH, 2, ROWS, SIZE), f32)],
        scratch=[
            pltpu.VMEM((SIZE, ROWS, SIZE), bf16),
            pltpu.VMEM((2 * SIZE, SIZE), bf16),
            pltpu.VMEM((2, FLAT, HALF), f32),
            pltpu.VMEM((SIZE, FLAT), bf16),
            pltpu.VMEM((2, FLAT, 2 * SIZE), bf16),
            pltpu.SemaphoreType.DMA((CHUNKS + 2,)),
        ],
        in_specs=[pl.BlockSpec(memory_space=pl.ANY)] * 3,
        out_specs=[pl.BlockSpec(memory_space=pltpu.VMEM)],
        grant=24,
        flops=6 << 29,
    )(in_hbm(iso), in_hbm(left), in_hbm(right))[0]


def prepare(iso, after):
    return call(
        prepare_kernel,
        "prepare",
        [pltpu.HBM((FLAT, SIZE), bf16), pltpu.HBM((SIZE, FLAT), bf16), square],
        scratch=[
            pltpu.VMEM((2, FLAT, HALF), f32),
            pltpu.VMEM((FLAT, SIZE), bf16),
            pltpu.VMEM((SIZE, FLAT), bf16),
            pltpu.SemaphoreType.DMA((2,)),
        ],
        ins=2,
        unread=1,
        flops=1 << 29,
    )(iso, after)


def rounded(got, *after):
    return call(round_kernel, "rounded", [((WIDTH, 2, ROWS, SIZE), bf16)], ins=3, unread=2)(got, *after)[0]


def first(index, own, near, couple, foreign):
    return call(first_kernel, "first", [kept, sliced], scratch=held, ins=5, smem=1)(
        index, own, near, couple, foreign
    )


def gradient(index, block, turned, edge, near, far, norm, after):
    return call(
        gradient_kernel,
        "gradient",
        [((SIZE, SIZE), bf16), ((WIDTH, 2 * ROWS + EXTRA, SIZE), bf16)],
        scratch=[
            pltpu.VMEM((FLAT, SIZE), bf16),
            pltpu.VMEM((SIZE, FLAT), bf16),
            pltpu.VMEM((FLAT, SIZE), bf16),
            pltpu.VMEM((SIZE, FLAT), bf16),
            pltpu.SemaphoreType.DMA((2 * CHUNKS,)),
        ],
        ins=8,
        smem=1,
        unread=3,
        flops=4 << 29,
        grant=20,
    )(index, in_hbm(edge), in_hbm(near), in_hbm(far), norm, in_hbm(block), in_hbm(turned), after)


def lines(mix, block, after):
    return call(
        lines_kernel,
        "lines",
        [pltpu.HBM((FLAT, SIZE), bf16), pltpu.HBM((FLAT, SIZE), bf16)],
        scratch=[
            pltpu.VMEM((2, FLAT, HALF), f32),
            pltpu.VMEM((FLAT, SIZE), bf16),
            pltpu.VMEM((FLAT, SIZE), bf16),
            pltpu.SemaphoreType.DMA((2,)),
        ],
        in_specs=[pl.BlockSpec(memory_space=pltpu.VMEM)] * 2 + [pl.BlockSpec(memory_space=pl.ANY)],
        out_specs=[pl.BlockSpec(memory_space=pl.ANY)] * 2,
        flops=1 << 29,
        grant=20,
    )(mix, block, after)


def pack(got, parts, foreign):
    return call(pack_kernel, "pack", [((WIDTH, 6 * ROWS + EXTRA, SIZE), bf16)], ins=3)(got, parts, foreign)[0]


def repeat(got, sums, after):
    return call(repeat_kernel, "repeat", [((WIDTH, 4 * ROWS, SIZE), bf16)], ins=3, unread=1)(
        got, sums, in_hbm(after)
    )[0]


def second(index, got, old, couple):
    return call(
        second_kernel,
        "second",
        [kept, sliced, ((2 * ROWS, SIZE), bf16), ((EXTRA, SIZE), f32)],
        scratch=held,
        ins=4,
        smem=1,
    )(index, got, in_hbm(old), couple)


def final(got, extra, old, couple, iso, hi, lo):
    vmem = pl.BlockSpec(memory_space=pltpu.VMEM)
    any_place = pl.BlockSpec(memory_space=pl.ANY)
    return call(
        final_kernel,
        "final",
        [pltpu.HBM((SIZE, SIZE), f32), pltpu.HBM(iso.shape, bf16)],
        scratch=[
            pltpu.VMEM((5 * SIZE, SIZE), bf16),
            pltpu.VMEM((FLAT, SIZE), bf16),
            pltpu.VMEM((FLAT, SIZE), bf16),
            pltpu.VMEM((SIZE, SIZE), f32),
            pltpu.VMEM((SIZE, ROWS, SIZE), bf16),
            pltpu.SemaphoreType.DMA((3 + PARTS,)),
        ],
        in_specs=[vmem] * 5 + [any_place] * 2,
        out_specs=[any_place] * 2,
        flops=5 << 29,
        grant=20,
    )(got, extra, in_hbm(old), couple, iso, in_hbm(hi), in_hbm(lo))


def body(iso, edge_left, edge_right, coupling):
    iso, left, right, couple = iso[0], edge_left[0], edge_right[0], coupling[0]
    s = lax.axis_index("blk")
    j = lax.axis_index("bond")
    z = s // 2
    index = jnp.stack([j, z % 4, s % 2, z // 4]).astype(jnp.int32)

    couple_1 = permuted(couple, "blk", lambda i: i ^ 2)
    part_2 = lax.dynamic_slice_in_dim(couple, j * ROWS, ROWS, 0)
    part_2 = permuted(part_2, "blk", lambda i: i ^ 8)

    blocks = ascend(iso, left, right)
    block, turned, norm = prepare(iso, blocks)
    share = rounded(exchange(blocks, "bond"), norm, part_2)
    own = exchange(share, "bond")
    near = permuted(own, "blk", lambda i: i ^ 1)
    far = permuted(own, "blk", lambda i: (i + 1) % 32 if i % 2 else (i - 1) % 32)

    quads = [[(zq * 4 + zl) * 2 + c for zl in range(4)] for zq in range(4) for c in range(2)]
    strides = [[(zh * 4 + zl) * 2 + c for zh in range(4)] for zl in range(4) for c in range(2)]

    env, outgoing = first(index, own, near, couple, couple_1)
    incoming = exchange(outgoing, "blk", quads)
    mix, parts = gradient(index, block, turned, left, near, far, norm, outgoing)
    got = exchange(pack(incoming, parts, part_2), "bond")
    env, outgoing, sums, extra = second(index, got, env, couple)
    incoming = exchange(outgoing, "blk", strides)
    moved_hi, moved_lo = lines(mix, block, outgoing)
    got = exchange(repeat(incoming, sums, moved_hi), "bond")
    env, out = final(got, extra, env, couple, iso, moved_hi, moved_lo)
    return (out[None], env[None])


def solution(mesh):
    placed = (
        P("blk", None, "bond", None),
        P("blk", None, None),
        P("blk", None, None),
        P("blk", None, None),
    )
    return jax.shard_map(
        body,
        mesh=mesh,
        in_specs=placed,
        out_specs=(P("blk", None, "bond", None), P("blk", None, None)),
        check_vma=False,
    )
```

```python
import jax
import jax.numpy as jnp
from jax import lax
from jax.experimental import pallas as pl
from jax.experimental.pallas import tpu as pltpu
from jax.sharding import PartitionSpec as P

bf16 = jnp.bfloat16
f32 = jnp.float32
NN = ((1,), (0,))
NT = ((1,), (1,))
SIZE = 256
WIDTH = 16
ROWS = SIZE // WIDTH
FLAT = SIZE * ROWS
HALF = 128
CHUNKS = 4
EXTRA = 8
PARTS = 2


def split(x):
    hi = x.astype(bf16)
    return hi, (x - hi.astype(f32)).astype(bf16)


def mm(a, b, dims=NN):
    return lax.dot_general(a, b, (dims, ((), ())), preferred_element_type=f32)


def mm3(a, b, dims=NN):
    ah, al = split(a)
    bh, bl = split(b)
    return mm(ah, bh, dims) + (mm(ah, bl, dims) + mm(al, bh, dims))


def sandwich(c, e):
    return mm3(mm3(c, e), c, NT)


def in_hbm(x):
    return pltpu.with_memory_space_constraint(x, pltpu.HBM)


def iotas():
    shape = (SIZE, SIZE)
    return lax.broadcasted_iota(jnp.int32, shape, 0), lax.broadcasted_iota(jnp.int32, shape, 1)


def call(kernel, name, outs, scratch=(), smem=0, unread=0, ins=0, flops=0, grant=16, grid=None, in_specs=None, out_specs=None):
    vmem = pl.BlockSpec(memory_space=pltpu.VMEM)
    any_place = pl.BlockSpec(memory_space=pl.ANY)
    if in_specs is None:
        in_specs = (
            [pl.BlockSpec(memory_space=pltpu.SMEM)] * smem
            + [vmem] * (ins - smem - unread)
            + [any_place] * unread
        )
        out_specs = [vmem] * len(outs)
    params = dict(grid=grid) if grid else {}
    return pl.pallas_call(
        kernel,
        name=name,
        out_shape=[o if isinstance(o, pl.MemoryRef) else jax.ShapeDtypeStruct(*o) for o in outs],
        in_specs=in_specs,
        out_specs=out_specs,
        scratch_shapes=scratch,
        compiler_params=pltpu.CompilerParams(vmem_limit_bytes=grant << 20),
        cost_estimate=pl.CostEstimate(flops=flops, bytes_accessed=4 << 20, transcendentals=0),
        **params,
    )


def spread_rows(iso_ref, wide_ref):
    wide = iso_ref[...].reshape(FLAT, SIZE).astype(f32)
    wide_ref[0] = wide[:, :HALF]
    wide_ref[1] = wide[:, HALF:]


def bond_slice(wide_ref, b):
    rows = pl.ds(b, SIZE, stride=ROWS)
    return jnp.concatenate([wide_ref[h, rows, :].astype(bf16) for h in range(2)], axis=1)


def ascend_kernel(iso_hbm, left_hbm, right_hbm, out_ref, iso_ref, edge_ref, wide_ref, turned_ref, mapped_ref, sems):
    step = SIZE // CHUNKS
    copies = []
    for i in range(CHUNKS):
        here = pl.ds(i * step, step)
        copies.append(pltpu.make_async_copy(iso_hbm.at[here], iso_ref.at[here], sems.at[i]))
    edge_copies = [
        pltpu.make_async_copy(left_hbm, edge_ref.at[pl.ds(0, SIZE)], sems.at[CHUNKS]),
        pltpu.make_async_copy(right_hbm, edge_ref.at[pl.ds(SIZE, SIZE)], sems.at[CHUNKS + 1]),
    ]
    for copy in copies + edge_copies:
        copy.start()
    for i, copy in enumerate(copies):
        copy.wait()
        wide = iso_ref[i * step : (i + 1) * step].reshape(step * ROWS, SIZE).astype(f32)
        for h in range(2):
            wide_ref[h, i * step * ROWS : (i + 1) * step * ROWS] = wide[:, h * HALF : (h + 1) * HALF]
    for copy in edge_copies:
        copy.wait()
    edges = edge_ref[...]
    for b in range(ROWS):
        block = bond_slice(wide_ref, b)
        here = slice(b * SIZE, (b + 1) * SIZE)
        turned_ref[:, here] = block.T
        for k, part in enumerate(split(mm(edges, block))):
            mapped_ref[k, here, :SIZE] = part[:SIZE]
            mapped_ref[k, here, SIZE:] = part[SIZE:]
    turned = turned_ref[...]
    total = mm(turned, mapped_ref[0]) + mm(turned, mapped_ref[1])
    for k in range(2):
        out_ref[:, k] = total[:, k * SIZE : (k + 1) * SIZE].reshape(WIDTH, ROWS, SIZE)


def prepare_kernel(iso_ref, after_ref, block_hbm, turned_hbm, norm_ref, wide_ref, block_ref, turned_ref, sems):
    spread_rows(iso_ref, wide_ref)
    for b in range(ROWS):
        block = bond_slice(wide_ref, b)
        here = slice(b * SIZE, (b + 1) * SIZE)
        block_ref[here] = block
        turned_ref[:, here] = block.T
    copies = [
        pltpu.make_async_copy(block_ref, block_hbm, sems.at[0]),
        pltpu.make_async_copy(turned_ref, turned_hbm, sems.at[1]),
    ]
    for copy in copies:
        copy.start()
    norm_ref[...] = mm(turned_ref[...], block_ref[...])
    for copy in copies:
        copy.wait()


def round_kernel(got_ref, after_ref, also_ref, out_ref):
    share = got_ref[0]
    for i in range(1, WIDTH):
        share = share + got_ref[i]
    share = share.astype(bf16)
    for i in range(WIDTH):
        out_ref[i] = share


def slices(index_ref, place, env_ref, left, foreign, out_ref):
    own = env_ref[pl.ds(index_ref[0] * ROWS, ROWS), :]
    crossed = mm3(mm3(left, env_ref[...]), foreign, NT)
    for p in range(4):
        which = index_ref[place] ^ p
        out_ref[p] = jnp.where(which == 3, crossed, jnp.where(which == 0, 0.0, own))


def first_kernel(index_ref, own_ref, near_ref, couple_ref, foreign_ref, env_ref, out_ref):
    def whole(ref):
        return (ref[:, 0].astype(f32) + ref[:, 1].astype(f32)).reshape(SIZE, SIZE)

    env_ref[...] = 0.5 * (whole(own_ref) + sandwich(couple_ref[...], whole(near_ref)))
    left = foreign_ref[pl.ds(index_ref[0] * ROWS, ROWS), :]
    slices(index_ref, 1, env_ref, left, foreign_ref[...], out_ref)


def gradient_kernel(index_ref, edge_ref, near_ref, far_ref, norm_ref, block_hbm, turned_hbm, after_ref, hi_hbm, lo_hbm, out_ref, moved_ref, low_ref, flipped_ref, block_ref, turned_ref, sems):
    copies = []
    step = FLAT // CHUNKS
    for i in range(CHUNKS):
        here = pl.ds(i * step, step)
        copies.append(pltpu.make_async_copy(block_hbm.at[here], block_ref.at[here], sems.at[2 * i]))
        copies.append(pltpu.make_async_copy(turned_hbm.at[:, here], turned_ref.at[:, here], sems.at[2 * i + 1]))
    for copy in copies:
        copy.start()
    odd = index_ref[2] == 1

    def whole(ref, k):
        return ref[:, k].astype(f32).reshape(SIZE, SIZE)

    from_left = jnp.where(odd, whole(near_ref, 1), whole(far_ref, 1))
    from_right = jnp.where(odd, whole(far_ref, 0), whole(near_ref, 0))
    mix = (edge_ref[...].astype(f32) + from_left + from_right).astype(bf16)
    squares = jnp.zeros((8, SIZE), f32)
    for b in range(ROWS):
        if b % (ROWS // CHUNKS) == 0:
            at = 2 * b // (ROWS // CHUNKS)
            copies[at].wait()
            copies[at + 1].wait()
        here = slice(b * SIZE, (b + 1) * SIZE)
        moved = mm(mix, block_ref[here])
        squares = squares + jnp.sum((moved * moved).reshape(SIZE // 8, 8, SIZE), axis=0)
        moved_ref[here], low_ref[here] = split(moved)
        flipped_ref[:, here] = mm(turned_ref[:, here], mix, NT).astype(bf16)
    outgoing = [
        pltpu.make_async_copy(moved_ref, hi_hbm, sems.at[2 * CHUNKS]),
        pltpu.make_async_copy(low_ref, lo_hbm, sems.at[2 * CHUNKS + 1]),
    ]
    for copy in outgoing:
        copy.start()
    part_q = mm(turned_ref[...], moved_ref[...])
    part_r = mm(flipped_ref[...], moved_ref[...])
    part_n = norm_ref[...]
    row, col = iotas()
    diag_n = jnp.sum(jnp.where(row == col, part_n, 0.0), axis=0, keepdims=True)
    diag_r = jnp.sum(squares, axis=0, keepdims=True)
    part_r = jnp.where(row == col, diag_r, part_r)
    nh, nl = split(diag_n)
    _, rl = split(diag_r)
    extra = jnp.concatenate(
        [nh.astype(f32), nl.astype(f32), rl.astype(f32), jnp.zeros((EXTRA - 3, SIZE), f32)], axis=0
    ).astype(bf16)
    packed = jnp.where(row < col, part_n, part_r)
    out_ref[:, :ROWS] = part_q.astype(bf16).reshape(WIDTH, ROWS, SIZE)
    out_ref[:, ROWS : 2 * ROWS] = packed.astype(bf16).reshape(WIDTH, ROWS, SIZE)
    for i in range(WIDTH):
        out_ref[i, 2 * ROWS :] = extra
    for copy in outgoing:
        copy.wait()


def pack_kernel(got_ref, parts_ref, foreign_ref, out_ref):
    hi, lo = split((got_ref[0] + got_ref[1]) + (got_ref[2] + got_ref[3]))
    foreign_hi, foreign_lo = split(foreign_ref[...])
    for i in range(WIDTH):
        out_ref[i, :ROWS] = hi
        out_ref[i, ROWS : 2 * ROWS] = lo
        out_ref[i, 4 * ROWS : 5 * ROWS] = foreign_hi
        out_ref[i, 5 * ROWS : 6 * ROWS] = foreign_lo
    out_ref[:, 2 * ROWS : 4 * ROWS] = parts_ref[:, : 2 * ROWS]
    out_ref[:, 6 * ROWS :] = parts_ref[:, 2 * ROWS :]


def repeat_kernel(got_ref, sums_ref, out_ref):
    hi, lo = split((got_ref[0] + got_ref[1]) + (got_ref[2] + got_ref[3]))
    for i in range(WIDTH):
        out_ref[i, :ROWS] = hi
        out_ref[i, ROWS : 2 * ROWS] = lo
        out_ref[i, 2 * ROWS :] = sums_ref[...]


def two_levels(env_ref, got_ref, couple_ref):
    force = got_ref[:, :ROWS].astype(f32) + got_ref[:, ROWS : 2 * ROWS].astype(f32)
    return 0.25 * (env_ref[...] + sandwich(couple_ref[...], force.reshape(SIZE, SIZE)))


def second_kernel(index_ref, got_ref, old_ref, couple_ref, env_ref, out_ref, sums_ref, extra_ref):
    env_ref[...] = two_levels(old_ref, got_ref, couple_ref)

    def foreign(at):
        hi, lo = slice(4 * ROWS, 5 * ROWS), slice(5 * ROWS, 6 * ROWS)
        return got_ref[at, hi].astype(f32) + got_ref[at, lo].astype(f32)

    left = foreign(index_ref[0])
    slices(index_ref, 3, env_ref, left, foreign(slice(None)).reshape(SIZE, SIZE), out_ref)

    def total(rows):
        value = got_ref[0, rows].astype(f32)
        for i in range(1, WIDTH):
            value = value + got_ref[i, rows].astype(f32)
        return value

    extra_ref[...] = total(slice(6 * ROWS, 6 * ROWS + EXTRA))
    sums_ref[...] = total(slice(2 * ROWS, 4 * ROWS)).astype(bf16)


def mm2(a, b, dims=NN):
    ah, al = split(a)
    return mm(ah, b, dims) + mm(al, b, dims)


def polar_matrices(env, full_q, full_s, extra_ref):
    row, col = iotas()
    on = row == col
    top = env.astype(bf16)
    lower = jnp.where(row > col, full_s, 0.0)
    upper = jnp.where(row < col, full_s, 0.0)
    full_n = upper + upper.T + jnp.where(on, extra_ref[0:1, :] + extra_ref[1:2, :], 0.0)
    full_r = lower + lower.T + jnp.where(on, full_s + extra_ref[2:3, :], 0.0)
    half = full_q + 0.5 * mm2(full_n, top)
    hh, hl = split(half)
    turned = top.T
    side = mm(turned, hh) + mm(turned, hl)
    gram = full_r + side + side.T
    trace = jnp.sum(jnp.where(on, gram, 0.0), keepdims=True)
    factor = lax.rsqrt(trace + 1e-06)
    g = gram * (factor * factor)
    g2 = mm3(g, g)
    eye = jnp.where(on, 1.0, 0.0)
    poly = 2.25 * eye - 2.4375 * g + mm3(g2, 1.6875 * eye - 0.5625 * g + 0.0625 * g2)
    poly = poly * factor
    ph, pl_ = split(poly)
    return ph, pl_, mm(top, ph) + mm(top, pl_)


def final_kernel(got_ref, extra_ref, old_ref, couple_ref, block_hbm, hi_hbm, lo_hbm, env_hbm, out_hbm, map_ref, block_ref, hi_ref, lo_ref, env_ref, wide_ref, out_ref, sems):
    incoming = [
        pltpu.make_async_copy(hi_hbm, hi_ref, sems.at[0]),
        pltpu.make_async_copy(lo_hbm, lo_ref, sems.at[1]),
        pltpu.make_async_copy(block_hbm, block_ref, sems.at[2]),
    ]
    for copy in incoming:
        copy.start()
    env = two_levels(old_ref, got_ref, couple_ref)
    env_ref[...] = env
    outgoing = [pltpu.make_async_copy(env_ref, env_hbm, sems.at[3])]
    outgoing[0].start()
    full_q = got_ref[:, 2 * ROWS : 3 * ROWS].astype(f32).reshape(SIZE, SIZE)
    full_s = got_ref[:, 3 * ROWS :].astype(f32).reshape(SIZE, SIZE)
    ph, pl_, low = polar_matrices(env, full_q, full_s, extra_ref)
    for k, part in enumerate((ph, ph, pl_, *split(low))):
        map_ref[k * SIZE : (k + 1) * SIZE] = part
    for copy in incoming:
        copy.wait()
    step = SIZE // PARTS
    for i in range(PARTS):
        for b in range(ROWS):
            here = pl.ds(b * SIZE + i * step, step)
            hi = hi_ref[here]
            flat = block_ref[here]
            rows = jnp.concatenate([hi, lo_ref[here], hi, flat, flat], axis=1)
            value = mm(rows, map_ref[...])
            for h in range(2):
                wide_ref[h, pl.ds(i * step * ROWS + b, step, stride=ROWS), :] = value[:, h * HALF : (h + 1) * HALF]
        lines = pl.ds(i * step * ROWS, step * ROWS)
        here = pl.ds(i * step, step)
        for h in range(2):
            part = wide_ref[h, lines].astype(bf16).reshape(step, ROWS, HALF)
            out_ref[here, :, h * HALF : (h + 1) * HALF] = part
        copy = pltpu.make_async_copy(out_ref.at[here], out_hbm.at[here], sems.at[4 + i])
        copy.start()
        outgoing.append(copy)
    for copy in outgoing:
        copy.wait()


def exchange(x, axis, groups=None):
    return lax.all_to_all(x, axis, 0, 0, axis_index_groups=groups, tiled=True)


def permuted(x, axis, route):
    return lax.ppermute(x, axis, [(i, route(i)) for i in range(lax.axis_size(axis))])


square = ((SIZE, SIZE), f32)
kept = pltpu.HBM((SIZE, SIZE), f32)
sliced = ((4, ROWS, SIZE), f32)


def ascend(iso, left, right):
    return call(
        ascend_kernel,
        "ascend",
        [((WIDTH, 2, ROWS, SIZE), f32)],
        scratch=[
            pltpu.VMEM((SIZE, ROWS, SIZE), bf16),
            pltpu.VMEM((2 * SIZE, SIZE), bf16),
            pltpu.VMEM((2, FLAT, HALF), f32),
            pltpu.VMEM((SIZE, FLAT), bf16),
            pltpu.VMEM((2, FLAT, 2 * SIZE), bf16),
            pltpu.SemaphoreType.DMA((CHUNKS + 2,)),
        ],
        in_specs=[pl.BlockSpec(memory_space=pl.ANY)] * 3,
        out_specs=[pl.BlockSpec(memory_space=pltpu.VMEM)],
        grant=24,
        flops=6 << 29,
    )(in_hbm(iso), in_hbm(left), in_hbm(right))[0]


def prepare(iso, after):
    return call(
        prepare_kernel,
        "prepare",
        [pltpu.HBM((FLAT, SIZE), bf16), pltpu.HBM((SIZE, FLAT), bf16), square],
        scratch=[
            pltpu.VMEM((2, FLAT, HALF), f32),
            pltpu.VMEM((FLAT, SIZE), bf16),
            pltpu.VMEM((SIZE, FLAT), bf16),
            pltpu.SemaphoreType.DMA((2,)),
        ],
        in_specs=[pl.BlockSpec(memory_space=pltpu.VMEM), pl.BlockSpec(memory_space=pl.ANY)],
        out_specs=[pl.BlockSpec(memory_space=pl.ANY)] * 2 + [pl.BlockSpec(memory_space=pltpu.VMEM)],
        flops=1 << 29,
    )(iso, after)


def rounded(got, *after):
    return call(round_kernel, "rounded", [((WIDTH, 2, ROWS, SIZE), bf16)], ins=3, unread=2)(got, *after)[0]


def first(index, own, near, couple, foreign):
    return call(first_kernel, "first", [kept, sliced], ins=5, smem=1)(
        index, own, near, couple, foreign
    )


def gradient(index, block, turned, edge, near, far, norm, after):
    vmem = pl.BlockSpec(memory_space=pltpu.VMEM)
    any_place = pl.BlockSpec(memory_space=pl.ANY)
    return call(
        gradient_kernel,
        "gradient",
        [pltpu.HBM((FLAT, SIZE), bf16), pltpu.HBM((FLAT, SIZE), bf16), ((WIDTH, 2 * ROWS + EXTRA, SIZE), bf16)],
        scratch=[
            pltpu.VMEM((FLAT, SIZE), bf16),
            pltpu.VMEM((FLAT, SIZE), bf16),
            pltpu.VMEM((SIZE, FLAT), bf16),
            pltpu.VMEM((FLAT, SIZE), bf16),
            pltpu.VMEM((SIZE, FLAT), bf16),
            pltpu.SemaphoreType.DMA((2 * CHUNKS + 2,)),
        ],
        in_specs=[pl.BlockSpec(memory_space=pltpu.SMEM)] + [vmem] * 4 + [any_place] * 3,
        out_specs=[any_place] * 2 + [vmem],
        flops=4 << 29,
        grant=20,
    )(index, in_hbm(edge), in_hbm(near), in_hbm(far), norm, in_hbm(block), in_hbm(turned), after)


def pack(got, parts, foreign):
    return call(pack_kernel, "pack", [((WIDTH, 6 * ROWS + EXTRA, SIZE), bf16)], ins=3)(got, parts, foreign)[0]


def repeat(got, sums):
    return call(repeat_kernel, "repeat", [((WIDTH, 4 * ROWS, SIZE), bf16)], ins=2)(got, sums)[0]


def second(index, got, old, couple):
    return call(
        second_kernel,
        "second",
        [square, sliced, ((2 * ROWS, SIZE), bf16), ((EXTRA, SIZE), f32)],
        ins=4,
        smem=1,
    )(index, got, in_hbm(old), couple)


def final(got, extra, old, couple, block, hi, lo):
    vmem = pl.BlockSpec(memory_space=pltpu.VMEM)
    any_place = pl.BlockSpec(memory_space=pl.ANY)
    return call(
        final_kernel,
        "final",
        [pltpu.HBM((SIZE, SIZE), f32), pltpu.HBM((SIZE, ROWS, SIZE), bf16)],
        scratch=[
            pltpu.VMEM((5 * SIZE, SIZE), bf16),
            pltpu.VMEM((FLAT, SIZE), bf16),
            pltpu.VMEM((FLAT, SIZE), bf16),
            pltpu.VMEM((FLAT, SIZE), bf16),
            pltpu.VMEM((SIZE, SIZE), f32),
            pltpu.VMEM((2, FLAT, HALF), f32),
            pltpu.VMEM((SIZE, ROWS, SIZE), bf16),
            pltpu.SemaphoreType.DMA((4 + PARTS,)),
        ],
        in_specs=[vmem] * 4 + [any_place] * 3,
        out_specs=[any_place] * 2,
        flops=5 << 29,
        grant=24,
    )(got, extra, old, couple, in_hbm(block), in_hbm(hi), in_hbm(lo))


def body(iso, edge_left, edge_right, coupling):
    iso, left, right, couple = iso[0], edge_left[0], edge_right[0], coupling[0]
    s = lax.axis_index("blk")
    j = lax.axis_index("bond")
    z = s // 2
    index = jnp.stack([j, z % 4, s % 2, z // 4]).astype(jnp.int32)

    couple_1 = permuted(couple, "blk", lambda i: i ^ 2)
    part_2 = lax.dynamic_slice_in_dim(couple, j * ROWS, ROWS, 0)
    part_2 = permuted(part_2, "blk", lambda i: i ^ 8)

    blocks = ascend(iso, left, right)
    block, turned, norm = prepare(iso, blocks)
    share = rounded(exchange(blocks, "bond"), norm, part_2)
    own = exchange(share, "bond")
    near = permuted(own, "blk", lambda i: i ^ 1)
    far = permuted(own, "blk", lambda i: (i + 1) % 32 if i % 2 else (i - 1) % 32)

    quads = [[(zq * 4 + zl) * 2 + c for zl in range(4)] for zq in range(4) for c in range(2)]
    strides = [[(zh * 4 + zl) * 2 + c for zh in range(4)] for zl in range(4) for c in range(2)]

    env, outgoing = first(index, own, near, couple, couple_1)
    incoming = exchange(outgoing, "blk", quads)
    moved_hi, moved_lo, parts = gradient(index, block, turned, left, near, far, norm, outgoing)
    got = exchange(pack(incoming, parts, part_2), "bond")
    env, outgoing, sums, extra = second(index, got, env, couple)
    incoming = exchange(outgoing, "blk", strides)
    got = exchange(repeat(incoming, sums), "bond")
    env, out = final(got, extra, env, couple, block, moved_hi, moved_lo)
    return (out[None], env[None])


def solution(mesh):
    placed = (
        P("blk", None, "bond", None),
        P("blk", None, None),
        P("blk", None, None),
        P("blk", None, None),
    )
    return jax.shard_map(
        body,
        mesh=mesh,
        in_specs=placed,
        out_specs=(P("blk", None, "bond", None), P("blk", None, None)),
        check_vma=False,
    )
```

```python
import jax
import jax.numpy as jnp
from jax import lax
from jax.experimental import pallas as pl
from jax.experimental.pallas import tpu as pltpu
from jax.sharding import PartitionSpec as P

bf16 = jnp.bfloat16
f32 = jnp.float32
NN = ((1,), (0,))
NT = ((1,), (1,))
SIZE = 256
WIDTH = 16
ROWS = SIZE // WIDTH
FLAT = SIZE * ROWS
HALF = 128
CHUNKS = 4
EXTRA = 8
PARTS = 2


def split(x):
    hi = x.astype(bf16)
    return hi, (x - hi.astype(f32)).astype(bf16)


def mm(a, b, dims=NN):
    return lax.dot_general(a, b, (dims, ((), ())), preferred_element_type=f32)


def mm3(a, b, dims=NN):
    ah, al = split(a)
    bh, bl = split(b)
    return mm(ah, bh, dims) + (mm(ah, bl, dims) + mm(al, bh, dims))


def sandwich(c, e):
    return mm3(mm3(c, e), c, NT)


def in_hbm(x):
    return pltpu.with_memory_space_constraint(x, pltpu.HBM)


def iotas():
    shape = (SIZE, SIZE)
    return lax.broadcasted_iota(jnp.int32, shape, 0), lax.broadcasted_iota(jnp.int32, shape, 1)


def call(kernel, name, outs, scratch=(), smem=0, unread=0, ins=0, flops=0, grant=16, grid=None, in_specs=None, out_specs=None):
    vmem = pl.BlockSpec(memory_space=pltpu.VMEM)
    any_place = pl.BlockSpec(memory_space=pl.ANY)
    if in_specs is None:
        in_specs = (
            [pl.BlockSpec(memory_space=pltpu.SMEM)] * smem
            + [vmem] * (ins - smem - unread)
            + [any_place] * unread
        )
        out_specs = [vmem] * len(outs)
    params = dict(grid=grid) if grid else {}
    return pl.pallas_call(
        kernel,
        name=name,
        out_shape=[o if isinstance(o, pl.MemoryRef) else jax.ShapeDtypeStruct(*o) for o in outs],
        in_specs=in_specs,
        out_specs=out_specs,
        scratch_shapes=scratch,
        compiler_params=pltpu.CompilerParams(vmem_limit_bytes=grant << 20),
        cost_estimate=pl.CostEstimate(flops=flops, bytes_accessed=4 << 20, transcendentals=0),
        **params,
    )


def spread_rows(iso_ref, wide_ref):
    wide = iso_ref[...].reshape(FLAT, SIZE).astype(f32)
    wide_ref[0] = wide[:, :HALF]
    wide_ref[1] = wide[:, HALF:]


def bond_slice(wide_ref, b):
    rows = pl.ds(b, SIZE, stride=ROWS)
    return jnp.concatenate([wide_ref[h, rows, :].astype(bf16) for h in range(2)], axis=1)


def ascend_kernel(iso_hbm, left_hbm, right_hbm, out_ref, iso_ref, edge_ref, wide_ref, turned_ref, mapped_ref, sems):
    step = SIZE // CHUNKS
    copies = []
    for i in range(CHUNKS):
        here = pl.ds(i * step, step)
        copies.append(pltpu.make_async_copy(iso_hbm.at[here], iso_ref.at[here], sems.at[i]))
    edge_copies = [
        pltpu.make_async_copy(left_hbm, edge_ref.at[pl.ds(0, SIZE)], sems.at[CHUNKS]),
        pltpu.make_async_copy(right_hbm, edge_ref.at[pl.ds(SIZE, SIZE)], sems.at[CHUNKS + 1]),
    ]
    for copy in copies + edge_copies:
        copy.start()
    for i, copy in enumerate(copies):
        copy.wait()
        wide = iso_ref[i * step : (i + 1) * step].reshape(step * ROWS, SIZE).astype(f32)
        for h in range(2):
            wide_ref[h, i * step * ROWS : (i + 1) * step * ROWS] = wide[:, h * HALF : (h + 1) * HALF]
    for copy in edge_copies:
        copy.wait()
    edges = edge_ref[...]
    total = jnp.zeros((SIZE, 2 * SIZE), f32)
    for b in range(ROWS + 2):
        if b < ROWS:
            block = bond_slice(wide_ref, b)
            here = slice(b * SIZE, (b + 1) * SIZE)
            turned_ref[:, here] = block.T
            for k, part in enumerate(split(mm(edges, block))):
                mapped_ref[k, here, :SIZE] = part[:SIZE]
                mapped_ref[k, here, SIZE:] = part[SIZE:]
        if b >= 2 and b % 2 == 1:
            past = slice((b - 3) * SIZE, (b - 1) * SIZE)
            turned = turned_ref[:, past]
            total = total + (mm(turned, mapped_ref[0, past]) + mm(turned, mapped_ref[1, past]))
    for k in range(2):
        out_ref[:, k] = total[:, k * SIZE : (k + 1) * SIZE].reshape(WIDTH, ROWS, SIZE)


def prepare_kernel(iso_ref, after_ref, block_hbm, turned_hbm, norm_ref, wide_ref, block_ref, turned_ref, sems):
    spread_rows(iso_ref, wide_ref)
    for b in range(ROWS):
        block = bond_slice(wide_ref, b)
        here = slice(b * SIZE, (b + 1) * SIZE)
        block_ref[here] = block
        turned_ref[:, here] = block.T
    copies = [
        pltpu.make_async_copy(block_ref, block_hbm, sems.at[0]),
        pltpu.make_async_copy(turned_ref, turned_hbm, sems.at[1]),
    ]
    for copy in copies:
        copy.start()
    norm_ref[...] = mm(turned_ref[...], block_ref[...])
    for copy in copies:
        copy.wait()


def round_kernel(got_ref, after_ref, also_ref, out_ref):
    share = got_ref[0]
    for i in range(1, WIDTH):
        share = share + got_ref[i]
    share = share.astype(bf16)
    for i in range(WIDTH):
        out_ref[i] = share


def slices(index_ref, place, env_ref, left, foreign, out_ref):
    own = env_ref[pl.ds(index_ref[0] * ROWS, ROWS), :]
    crossed = mm3(mm3(left, env_ref[...]), foreign, NT)
    for p in range(4):
        which = index_ref[place] ^ p
        out_ref[p] = jnp.where(which == 3, crossed, jnp.where(which == 0, 0.0, own))


def first_kernel(index_ref, own_ref, near_ref, couple_ref, foreign_ref, env_ref, out_ref):
    def whole(ref):
        return (ref[:, 0].astype(f32) + ref[:, 1].astype(f32)).reshape(SIZE, SIZE)

    env_ref[...] = 0.5 * (whole(own_ref) + sandwich(couple_ref[...], whole(near_ref)))
    left = foreign_ref[pl.ds(index_ref[0] * ROWS, ROWS), :]
    slices(index_ref, 1, env_ref, left, foreign_ref[...], out_ref)


def gradient_kernel(index_ref, edge_ref, near_ref, far_ref, norm_ref, block_hbm, turned_hbm, after_ref, hi_hbm, lo_hbm, out_ref, moved_ref, low_ref, flipped_ref, block_ref, turned_ref, sems):
    copies = []
    step = FLAT // CHUNKS
    for i in range(CHUNKS):
        here = pl.ds(i * step, step)
        copies.append(pltpu.make_async_copy(block_hbm.at[here], block_ref.at[here], sems.at[2 * i]))
        copies.append(pltpu.make_async_copy(turned_hbm.at[:, here], turned_ref.at[:, here], sems.at[2 * i + 1]))
    for copy in copies:
        copy.start()
    odd = index_ref[2] == 1

    def whole(ref, k):
        return ref[:, k].astype(f32).reshape(SIZE, SIZE)

    from_left = jnp.where(odd, whole(near_ref, 1), whole(far_ref, 1))
    from_right = jnp.where(odd, whole(far_ref, 0), whole(near_ref, 0))
    mix = (edge_ref[...].astype(f32) + from_left + from_right).astype(bf16)
    squares = jnp.zeros((8, SIZE), f32)
    outgoing = []
    for b in range(ROWS):
        i, first_of = divmod(b, ROWS // CHUNKS)
        if first_of == 0:
            copies[2 * i].wait()
            copies[2 * i + 1].wait()
        here = slice(b * SIZE, (b + 1) * SIZE)
        moved = mm(mix, block_ref[here])
        squares = squares + jnp.sum((moved * moved).reshape(SIZE // 8, 8, SIZE), axis=0)
        moved_ref[here], low_ref[here] = split(moved)
        flipped_ref[:, here] = mm(turned_ref[:, here], mix, NT).astype(bf16)
        if first_of == ROWS // CHUNKS - 1:
            here = pl.ds(i * step, step)
            for k, (ref, hbm) in enumerate(((moved_ref, hi_hbm), (low_ref, lo_hbm))):
                copy = pltpu.make_async_copy(ref.at[here], hbm.at[here], sems.at[2 * (CHUNKS + i) + k])
                copy.start()
                outgoing.append(copy)
    part_q = mm(turned_ref[...], moved_ref[...])
    part_r = mm(flipped_ref[...], moved_ref[...])
    part_n = norm_ref[...]
    row, col = iotas()
    diag_n = jnp.sum(jnp.where(row == col, part_n, 0.0), axis=0, keepdims=True)
    diag_r = jnp.sum(squares, axis=0, keepdims=True)
    part_r = jnp.where(row == col, diag_r, part_r)
    nh, nl = split(diag_n)
    _, rl = split(diag_r)
    extra = jnp.concatenate(
        [nh.astype(f32), nl.astype(f32), rl.astype(f32), jnp.zeros((EXTRA - 3, SIZE), f32)], axis=0
    ).astype(bf16)
    packed = jnp.where(row < col, part_n, part_r)
    out_ref[:, :ROWS] = part_q.astype(bf16).reshape(WIDTH, ROWS, SIZE)
    out_ref[:, ROWS : 2 * ROWS] = packed.astype(bf16).reshape(WIDTH, ROWS, SIZE)
    for i in range(WIDTH):
        out_ref[i, 2 * ROWS :] = extra
    for copy in outgoing:
        copy.wait()


def pack_kernel(got_ref, parts_ref, foreign_ref, out_ref):
    hi, lo = split((got_ref[0] + got_ref[1]) + (got_ref[2] + got_ref[3]))
    foreign_hi, foreign_lo = split(foreign_ref[...])
    for i in range(WIDTH):
        out_ref[i, :ROWS] = hi
        out_ref[i, ROWS : 2 * ROWS] = lo
        out_ref[i, 4 * ROWS : 5 * ROWS] = foreign_hi
        out_ref[i, 5 * ROWS : 6 * ROWS] = foreign_lo
    out_ref[:, 2 * ROWS : 4 * ROWS] = parts_ref[:, : 2 * ROWS]
    out_ref[:, 6 * ROWS :] = parts_ref[:, 2 * ROWS :]


def repeat_kernel(got_ref, sums_ref, out_ref):
    hi, lo = split((got_ref[0] + got_ref[1]) + (got_ref[2] + got_ref[3]))
    for i in range(WIDTH):
        out_ref[i, :ROWS] = hi
        out_ref[i, ROWS : 2 * ROWS] = lo
        out_ref[i, 2 * ROWS :] = sums_ref[...]


def two_levels(env_ref, got_ref, couple_ref):
    force = got_ref[:, :ROWS].astype(f32) + got_ref[:, ROWS : 2 * ROWS].astype(f32)
    return 0.25 * (env_ref[...] + sandwich(couple_ref[...], force.reshape(SIZE, SIZE)))


def second_kernel(index_ref, got_ref, old_ref, couple_ref, env_ref, out_ref, sums_ref, extra_ref):
    env_ref[...] = two_levels(old_ref, got_ref, couple_ref)

    def foreign(at):
        hi, lo = slice(4 * ROWS, 5 * ROWS), slice(5 * ROWS, 6 * ROWS)
        return got_ref[at, hi].astype(f32) + got_ref[at, lo].astype(f32)

    left = foreign(index_ref[0])
    slices(index_ref, 3, env_ref, left, foreign(slice(None)).reshape(SIZE, SIZE), out_ref)

    def total(rows):
        value = got_ref[0, rows].astype(f32)
        for i in range(1, WIDTH):
            value = value + got_ref[i, rows].astype(f32)
        return value

    extra_ref[...] = total(slice(6 * ROWS, 6 * ROWS + EXTRA))
    sums_ref[...] = total(slice(2 * ROWS, 4 * ROWS)).astype(bf16)


def mm2(a, b, dims=NN):
    ah, al = split(a)
    return mm(ah, b, dims) + mm(al, b, dims)


def polar_matrices(env, full_q, full_s, extra_ref):
    row, col = iotas()
    on = row == col
    top = env.astype(bf16)
    lower = jnp.where(row > col, full_s, 0.0)
    upper = jnp.where(row < col, full_s, 0.0)
    full_n = upper + upper.T + jnp.where(on, extra_ref[0:1, :] + extra_ref[1:2, :], 0.0)
    full_r = lower + lower.T + jnp.where(on, full_s + extra_ref[2:3, :], 0.0)
    half = full_q + 0.5 * mm2(full_n, top)
    hh, hl = split(half)
    turned = top.T
    side = mm(turned, hh) + mm(turned, hl)
    gram = full_r + side + side.T
    trace = jnp.sum(jnp.where(on, gram, 0.0), keepdims=True)
    factor = lax.rsqrt(trace + 1e-06)
    g = gram * (factor * factor)
    g2 = mm3(g, g)
    eye = jnp.where(on, 1.0, 0.0)
    poly = 2.25 * eye - 2.4375 * g + mm3(g2, 1.6875 * eye - 0.5625 * g + 0.0625 * g2)
    poly = poly * factor
    ph, pl_ = split(poly)
    return ph, pl_, mm(top, ph) + mm(top, pl_)


def final_kernel(got_ref, extra_ref, old_ref, couple_ref, hi_ref, lo_ref, block_hbm, env_hbm, out_hbm, map_ref, env_ref, block_ref, wide_ref, out_ref, sems):
    incoming = pltpu.make_async_copy(block_hbm, block_ref, sems.at[1 + PARTS])
    incoming.start()
    env = two_levels(old_ref, got_ref, couple_ref)
    env_ref[...] = env
    outgoing = [pltpu.make_async_copy(env_ref, env_hbm, sems.at[0])]
    outgoing[0].start()
    full_q = got_ref[:, 2 * ROWS : 3 * ROWS].astype(f32).reshape(SIZE, SIZE)
    full_s = got_ref[:, 3 * ROWS :].astype(f32).reshape(SIZE, SIZE)
    ph, pl_, low = polar_matrices(env, full_q, full_s, extra_ref)
    for k, part in enumerate((ph, ph, pl_, *split(low))):
        map_ref[k * SIZE : (k + 1) * SIZE] = part
    incoming.wait()
    step = SIZE // PARTS
    for i in range(PARTS):
        for b in range(ROWS):
            here = pl.ds(b * SIZE + i * step, step)
            hi = hi_ref[here]
            flat = block_ref[here]
            rows = jnp.concatenate([hi, lo_ref[here], hi, flat, flat], axis=1)
            value = mm(rows, map_ref[...])
            for h in range(2):
                wide_ref[h, pl.ds(i * step * ROWS + b, step, stride=ROWS), :] = value[:, h * HALF : (h + 1) * HALF]
        lines = pl.ds(i * step * ROWS, step * ROWS)
        here = pl.ds(i * step, step)
        for h in range(2):
            part = wide_ref[h, lines].astype(bf16).reshape(step, ROWS, HALF)
            out_ref[here, :, h * HALF : (h + 1) * HALF] = part
        copy = pltpu.make_async_copy(out_ref.at[here], out_hbm.at[here], sems.at[1 + i])
        copy.start()
        outgoing.append(copy)
    for copy in outgoing:
        copy.wait()


def exchange(x, axis, groups=None):
    return lax.all_to_all(x, axis, 0, 0, axis_index_groups=groups, tiled=True)


def permuted(x, axis, route):
    return lax.ppermute(x, axis, [(i, route(i)) for i in range(lax.axis_size(axis))])


square = ((SIZE, SIZE), f32)
kept = pltpu.HBM((SIZE, SIZE), f32)
sliced = ((4, ROWS, SIZE), f32)


def ascend(iso, left, right):
    return call(
        ascend_kernel,
        "ascend",
        [((WIDTH, 2, ROWS, SIZE), f32)],
        scratch=[
            pltpu.VMEM((SIZE, ROWS, SIZE), bf16),
            pltpu.VMEM((2 * SIZE, SIZE), bf16),
            pltpu.VMEM((2, FLAT, HALF), f32),
            pltpu.VMEM((SIZE, FLAT), bf16),
            pltpu.VMEM((2, FLAT, 2 * SIZE), bf16),
            pltpu.SemaphoreType.DMA((CHUNKS + 2,)),
        ],
        in_specs=[pl.BlockSpec(memory_space=pl.ANY)] * 3,
        out_specs=[pl.BlockSpec(memory_space=pltpu.VMEM)],
        grant=24,
        flops=6 << 29,
    )(in_hbm(iso), in_hbm(left), in_hbm(right))[0]


def prepare(iso, after):
    return call(
        prepare_kernel,
        "prepare",
        [pltpu.HBM((FLAT, SIZE), bf16), pltpu.HBM((SIZE, FLAT), bf16), square],
        scratch=[
            pltpu.VMEM((2, FLAT, HALF), f32),
            pltpu.VMEM((FLAT, SIZE), bf16),
            pltpu.VMEM((SIZE, FLAT), bf16),
            pltpu.SemaphoreType.DMA((2,)),
        ],
        in_specs=[pl.BlockSpec(memory_space=pltpu.VMEM), pl.BlockSpec(memory_space=pl.ANY)],
        out_specs=[pl.BlockSpec(memory_space=pl.ANY)] * 2 + [pl.BlockSpec(memory_space=pltpu.VMEM)],
        flops=1 << 29,
    )(iso, after)


def rounded(got, *after):
    return call(round_kernel, "rounded", [((WIDTH, 2, ROWS, SIZE), bf16)], ins=3, unread=2)(got, *after)[0]


def first(index, own, near, couple, foreign):
    return call(first_kernel, "first", [kept, sliced], ins=5, smem=1)(
        index, own, near, couple, foreign
    )


def gradient(index, block, turned, edge, near, far, norm, after):
    vmem = pl.BlockSpec(memory_space=pltpu.VMEM)
    any_place = pl.BlockSpec(memory_space=pl.ANY)
    return call(
        gradient_kernel,
        "gradient",
        [pltpu.HBM((FLAT, SIZE), bf16), pltpu.HBM((FLAT, SIZE), bf16), ((WIDTH, 2 * ROWS + EXTRA, SIZE), bf16)],
        scratch=[
            pltpu.VMEM((FLAT, SIZE), bf16),
            pltpu.VMEM((FLAT, SIZE), bf16),
            pltpu.VMEM((SIZE, FLAT), bf16),
            pltpu.VMEM((FLAT, SIZE), bf16),
            pltpu.VMEM((SIZE, FLAT), bf16),
            pltpu.SemaphoreType.DMA((4 * CHUNKS,)),
        ],
        in_specs=[pl.BlockSpec(memory_space=pltpu.SMEM)] + [vmem] * 4 + [any_place] * 3,
        out_specs=[any_place] * 2 + [vmem],
        flops=4 << 29,
        grant=20,
    )(index, in_hbm(edge), in_hbm(near), far, norm, in_hbm(block), in_hbm(turned), after)


def pack(got, parts, foreign):
    return call(pack_kernel, "pack", [((WIDTH, 6 * ROWS + EXTRA, SIZE), bf16)], ins=3)(got, parts, foreign)[0]


def repeat(got, sums):
    return call(repeat_kernel, "repeat", [((WIDTH, 4 * ROWS, SIZE), bf16)], ins=2)(got, sums)[0]


def second(index, got, old, couple):
    return call(
        second_kernel,
        "second",
        [square, sliced, ((2 * ROWS, SIZE), bf16), ((EXTRA, SIZE), f32)],
        ins=4,
        smem=1,
    )(index, got, in_hbm(old), couple)


def final(got, extra, old, couple, hi, lo, block):
    vmem = pl.BlockSpec(memory_space=pltpu.VMEM)
    any_place = pl.BlockSpec(memory_space=pl.ANY)
    return call(
        final_kernel,
        "final",
        [pltpu.HBM((SIZE, SIZE), f32), pltpu.HBM((SIZE, ROWS, SIZE), bf16)],
        scratch=[
            pltpu.VMEM((5 * SIZE, SIZE), bf16),
            pltpu.VMEM((SIZE, SIZE), f32),
            pltpu.VMEM((FLAT, SIZE), bf16),
            pltpu.VMEM((2, FLAT, HALF), f32),
            pltpu.VMEM((SIZE, ROWS, SIZE), bf16),
            pltpu.SemaphoreType.DMA((2 + PARTS,)),
        ],
        in_specs=[vmem] * 6 + [any_place],
        out_specs=[any_place] * 2,
        flops=5 << 29,
        grant=20,
    )(got, extra, old, couple, hi, lo, in_hbm(block))


def body(iso, edge_left, edge_right, coupling):
    iso, left, right, couple = iso[0], edge_left[0], edge_right[0], coupling[0]
    s = lax.axis_index("blk")
    j = lax.axis_index("bond")
    z = s // 2
    index = jnp.stack([j, z % 4, s % 2, z // 4]).astype(jnp.int32)

    couple_1 = permuted(couple, "blk", lambda i: i ^ 2)
    part_2 = lax.dynamic_slice_in_dim(couple, j * ROWS, ROWS, 0)
    part_2 = permuted(part_2, "blk", lambda i: i ^ 8)

    blocks = ascend(iso, left, right)
    block, turned, norm = prepare(iso, blocks)
    share = rounded(exchange(blocks, "bond"), norm, part_2)
    own = exchange(share, "bond")
    near = permuted(own, "blk", lambda i: i ^ 1)
    far = permuted(own, "blk", lambda i: (i + 1) % 32 if i % 2 else (i - 1) % 32)

    quads = [[(zq * 4 + zl) * 2 + c for zl in range(4)] for zq in range(4) for c in range(2)]
    strides = [[(zh * 4 + zl) * 2 + c for zh in range(4)] for zl in range(4) for c in range(2)]

    env, outgoing = first(index, own, near, couple, couple_1)
    incoming = exchange(outgoing, "blk", quads)
    moved_hi, moved_lo, parts = gradient(index, block, turned, left, near, far, norm, outgoing)
    got = exchange(pack(incoming, parts, part_2), "bond")
    env, outgoing, sums, extra = second(index, got, env, couple)
    incoming = exchange(outgoing, "blk", strides)
    got = exchange(repeat(incoming, sums), "bond")
    env, out = final(got, extra, env, couple, moved_hi, moved_lo, block)
    return (out[None], env[None])


def solution(mesh):
    placed = (
        P("blk", None, "bond", None),
        P("blk", None, None),
        P("blk", None, None),
        P("blk", None, None),
    )
    return jax.shard_map(
        body,
        mesh=mesh,
        in_specs=placed,
        out_specs=(P("blk", None, "bond", None), P("blk", None, None)),
        check_vma=False,
    )
```

```python
import jax
import jax.numpy as jnp
from jax import lax
from jax.experimental import pallas as pl
from jax.experimental.pallas import tpu as pltpu
from jax.sharding import PartitionSpec as P

bf16 = jnp.bfloat16
f32 = jnp.float32
NN = ((1,), (0,))
NT = ((1,), (1,))
SIZE = 256
WIDTH = 16
ROWS = SIZE // WIDTH
FLAT = SIZE * ROWS
HALF = 128
CHUNKS = 4
EXTRA = 8
PARTS = 2
TOGETHER = 8
SENDS = 4
NEAR = 0.01


def split(x):
    hi = x.astype(bf16)
    return hi, (x - hi.astype(f32)).astype(bf16)


def mm(a, b, dims=NN):
    return lax.dot_general(a, b, (dims, ((), ())), preferred_element_type=f32)


def mm3(a, b, dims=NN):
    ah, al = split(a)
    bh, bl = split(b)
    rows = jnp.concatenate([ah, ah, al], axis=1)
    return mm(rows, jnp.concatenate([bh, bl, bh], axis=dims[1][0]), dims)


def sandwich(c, e):
    return mm3(mm3(c, e), c, NT)


def in_hbm(x):
    return pltpu.with_memory_space_constraint(x, pltpu.HBM)


def iotas():
    shape = (SIZE, SIZE)
    return lax.broadcasted_iota(jnp.int32, shape, 0), lax.broadcasted_iota(jnp.int32, shape, 1)


def call(kernel, name, outs, scratch=(), smem=0, unread=0, ins=0, flops=0, grant=16, grid=None, in_specs=None, out_specs=None):
    vmem = pl.BlockSpec(memory_space=pltpu.VMEM)
    any_place = pl.BlockSpec(memory_space=pl.ANY)
    if in_specs is None:
        in_specs = (
            [pl.BlockSpec(memory_space=pltpu.SMEM)] * smem
            + [vmem] * (ins - smem - unread)
            + [any_place] * unread
        )
        out_specs = [vmem] * len(outs)
    params = dict(grid=grid) if grid else {}
    return pl.pallas_call(
        kernel,
        name=name,
        out_shape=[o if isinstance(o, pl.MemoryRef) else jax.ShapeDtypeStruct(*o) for o in outs],
        in_specs=in_specs,
        out_specs=out_specs,
        scratch_shapes=scratch,
        compiler_params=pltpu.CompilerParams(vmem_limit_bytes=grant << 20),
        cost_estimate=pl.CostEstimate(flops=flops, bytes_accessed=4 << 20, transcendentals=0),
        **params,
    )


def spread_rows(iso_ref, wide_ref):
    wide = iso_ref[...].reshape(FLAT, SIZE).astype(f32)
    wide_ref[0] = wide[:, :HALF]
    wide_ref[1] = wide[:, HALF:]


def bond_slice(wide_ref, b):
    rows = pl.ds(b, SIZE, stride=ROWS)
    return jnp.concatenate([wide_ref[h, rows, :].astype(bf16) for h in range(2)], axis=1)


def ascend_kernel(iso_hbm, left_hbm, right_hbm, out_ref, iso_ref, edge_ref, wide_ref, turned_ref, mapped_ref, sems):
    step = SIZE // CHUNKS
    copies = []
    for i in range(CHUNKS):
        here = pl.ds(i * step, step)
        copies.append(pltpu.make_async_copy(iso_hbm.at[here], iso_ref.at[here], sems.at[i]))
    edge_copies = [
        pltpu.make_async_copy(left_hbm, edge_ref.at[pl.ds(0, SIZE)], sems.at[CHUNKS]),
        pltpu.make_async_copy(right_hbm, edge_ref.at[pl.ds(SIZE, SIZE)], sems.at[CHUNKS + 1]),
    ]
    for copy in copies + edge_copies:
        copy.start()
    for i, copy in enumerate(copies):
        copy.wait()
        wide = iso_ref[i * step : (i + 1) * step].reshape(step * ROWS, SIZE).astype(f32)
        for h in range(2):
            wide_ref[h, i * step * ROWS : (i + 1) * step * ROWS] = wide[:, h * HALF : (h + 1) * HALF]
    for copy in edge_copies:
        copy.wait()
    edges = edge_ref[...]
    total = jnp.zeros((SIZE, 2 * SIZE), f32)
    for b in range(ROWS + 2):
        if b < ROWS:
            block = bond_slice(wide_ref, b)
            here = slice(b * SIZE, (b + 1) * SIZE)
            turned_ref[:, here] = block.T
            for k, part in enumerate(split(mm(edges, block))):
                mapped_ref[k, here, :SIZE] = part[:SIZE]
                mapped_ref[k, here, SIZE:] = part[SIZE:]
        if b >= 2 and b % 2 == 1:
            past = slice((b - 3) * SIZE, (b - 1) * SIZE)
            turned = turned_ref[:, past]
            total = total + (mm(turned, mapped_ref[0, past]) + mm(turned, mapped_ref[1, past]))
    for k in range(2):
        out_ref[:, k] = total[:, k * SIZE : (k + 1) * SIZE].reshape(WIDTH, ROWS, SIZE)


def prepare_kernel(iso_ref, after_ref, block_hbm, turned_hbm, norm_ref, wide_ref, block_ref, turned_ref, sems):
    spread_rows(iso_ref, wide_ref)
    for b in range(ROWS):
        block = bond_slice(wide_ref, b)
        here = slice(b * SIZE, (b + 1) * SIZE)
        block_ref[here] = block
        turned_ref[:, here] = block.T
    copies = [
        pltpu.make_async_copy(block_ref, block_hbm, sems.at[0]),
        pltpu.make_async_copy(turned_ref, turned_hbm, sems.at[1]),
    ]
    for copy in copies:
        copy.start()
    norm_ref[...] = mm(turned_ref[...], block_ref[...])
    for copy in copies:
        copy.wait()


def round_kernel(got_ref, after_ref, also_ref, out_ref):
    share = got_ref[0]
    for i in range(1, WIDTH):
        share = share + got_ref[i]
    share = share.astype(bf16)
    for i in range(WIDTH):
        out_ref[i] = share


def slices(index_ref, place, env_ref, left, foreign, out_ref):
    own = env_ref[pl.ds(index_ref[0] * ROWS, ROWS), :]
    crossed = mm3(mm3(left, env_ref[...]), foreign, NT)
    for p in range(4):
        which = index_ref[place] ^ p
        out_ref[p] = jnp.where(which == 3, crossed, jnp.where(which == 0, 0.0, own))


def first_kernel(index_ref, own_ref, near_ref, couple_ref, foreign_ref, env_ref, out_ref):
    def whole(ref):
        return (ref[:, 0].astype(f32) + ref[:, 1].astype(f32)).reshape(SIZE, SIZE)

    env_ref[...] = 0.5 * (whole(own_ref) + sandwich(couple_ref[...], whole(near_ref)))
    left = foreign_ref[pl.ds(index_ref[0] * ROWS, ROWS), :]
    slices(index_ref, 1, env_ref, left, foreign_ref[...], out_ref)


def gradient_kernel(index_ref, edge_ref, near_ref, far_ref, norm_ref, block_hbm, turned_hbm, after_ref, hi_hbm, lo_hbm, out_ref, moved_ref, low_ref, flipped_ref, block_ref, turned_ref, sems):
    copies = []
    step = FLAT // CHUNKS
    for i in range(CHUNKS):
        here = pl.ds(i * step, step)
        copies.append(pltpu.make_async_copy(block_hbm.at[here], block_ref.at[here], sems.at[2 * i]))
        copies.append(pltpu.make_async_copy(turned_hbm.at[:, here], turned_ref.at[:, here], sems.at[2 * i + 1]))
    for copy in copies:
        copy.start()
    odd = index_ref[2] == 1

    def whole(ref, k):
        return ref[:, k].astype(f32).reshape(SIZE, SIZE)

    from_left = jnp.where(odd, whole(near_ref, 1), whole(far_ref, 1))
    from_right = jnp.where(odd, whole(far_ref, 0), whole(near_ref, 0))
    mix = (edge_ref[...].astype(f32) + from_left + from_right).astype(bf16)
    squares = jnp.zeros((8, SIZE), f32)
    outgoing = []
    for b in range(ROWS):
        i, first_of = divmod(b, ROWS // CHUNKS)
        if first_of == 0:
            copies[2 * i].wait()
            copies[2 * i + 1].wait()
        here = slice(b * SIZE, (b + 1) * SIZE)
        moved = mm(mix, block_ref[here])
        squares = squares + jnp.sum((moved * moved).reshape(SIZE // 8, 8, SIZE), axis=0)
        moved_ref[here], low_ref[here] = split(moved)
        flipped_ref[:, here] = mm(turned_ref[:, here], mix, NT).astype(bf16)
        if first_of == ROWS // CHUNKS - 1:
            here = pl.ds(i * step, step)
            for k, (ref, hbm) in enumerate(((moved_ref, hi_hbm), (low_ref, lo_hbm))):
                copy = pltpu.make_async_copy(ref.at[here], hbm.at[here], sems.at[2 * (CHUNKS + i) + k])
                copy.start()
                outgoing.append(copy)
    part_q = mm(turned_ref[...], moved_ref[...])
    part_r = mm(flipped_ref[...], moved_ref[...])
    part_n = norm_ref[...]
    row, col = iotas()
    diag_n = jnp.sum(jnp.where(row == col, part_n, 0.0), axis=0, keepdims=True)
    diag_r = jnp.sum(squares, axis=0, keepdims=True)
    part_r = jnp.where(row == col, diag_r, part_r)
    nh, nl = split(diag_n)
    _, rl = split(diag_r)
    extra = jnp.concatenate(
        [nh.astype(f32), nl.astype(f32), rl.astype(f32), jnp.zeros((EXTRA - 3, SIZE), f32)], axis=0
    ).astype(bf16)
    packed = jnp.where(row < col, part_n, part_r)
    out_ref[:, :ROWS] = part_q.astype(bf16).reshape(WIDTH, ROWS, SIZE)
    out_ref[:, ROWS : 2 * ROWS] = packed.astype(bf16).reshape(WIDTH, ROWS, SIZE)
    for i in range(WIDTH):
        out_ref[i, 2 * ROWS :] = extra
    for copy in outgoing:
        copy.wait()


def pack_kernel(got_ref, parts_ref, foreign_ref, out_ref):
    hi, lo = split((got_ref[0] + got_ref[1]) + (got_ref[2] + got_ref[3]))
    foreign_hi, foreign_lo = split(foreign_ref[...])
    for i in range(WIDTH):
        out_ref[i, :ROWS] = hi
        out_ref[i, ROWS : 2 * ROWS] = lo
        out_ref[i, 4 * ROWS : 5 * ROWS] = foreign_hi
        out_ref[i, 5 * ROWS : 6 * ROWS] = foreign_lo
    out_ref[:, 2 * ROWS : 4 * ROWS] = parts_ref[:, : 2 * ROWS]
    out_ref[:, 6 * ROWS :] = parts_ref[:, 2 * ROWS :]


def repeat_kernel(got_ref, sums_ref, out_ref):
    hi, lo = split((got_ref[0] + got_ref[1]) + (got_ref[2] + got_ref[3]))
    for i in range(WIDTH):
        out_ref[i, :ROWS] = hi
        out_ref[i, ROWS : 2 * ROWS] = lo
        out_ref[i, 2 * ROWS :] = sums_ref[...]


def two_levels(env_ref, got_ref, couple_ref):
    force = got_ref[:, :ROWS].astype(f32) + got_ref[:, ROWS : 2 * ROWS].astype(f32)
    return 0.25 * (env_ref[...] + sandwich(couple_ref[...], force.reshape(SIZE, SIZE)))


def second_kernel(index_ref, got_ref, old_ref, couple_ref, env_ref, out_ref, sums_ref, extra_ref):
    env_ref[...] = two_levels(old_ref, got_ref, couple_ref)

    def foreign(at):
        hi, lo = slice(4 * ROWS, 5 * ROWS), slice(5 * ROWS, 6 * ROWS)
        return got_ref[at, hi].astype(f32) + got_ref[at, lo].astype(f32)

    left = foreign(index_ref[0])
    slices(index_ref, 3, env_ref, left, foreign(slice(None)).reshape(SIZE, SIZE), out_ref)

    def total(rows):
        value = got_ref[0, rows].astype(f32)
        for i in range(1, WIDTH):
            value = value + got_ref[i, rows].astype(f32)
        return value

    extra_ref[...] = total(slice(6 * ROWS, 6 * ROWS + EXTRA))
    sums_ref[...] = total(slice(2 * ROWS, 4 * ROWS)).astype(bf16)


def mm2(a, b, dims=NN):
    ah, al = split(a)
    return mm(jnp.concatenate([ah, al], axis=1), jnp.concatenate([b, b], axis=0), dims)


def polar_matrices(env, full_q, full_s, extra_ref):
    row, col = iotas()
    on = row == col
    top = env.astype(bf16)
    lower = jnp.where(row > col, full_s, 0.0)
    upper = jnp.where(row < col, full_s, 0.0)
    full_n = upper + upper.T + jnp.where(on, extra_ref[0:1, :] + extra_ref[1:2, :], 0.0)
    full_r = lower + lower.T + jnp.where(on, full_s + extra_ref[2:3, :], 0.0)
    half = full_q + 0.5 * mm2(full_n, top)
    hh, hl = split(half)
    turned = top.T
    side = mm(jnp.concatenate([turned, turned], axis=1), jnp.concatenate([hh, hl], axis=0))
    gram = full_r + side + side.T
    trace = jnp.sum(jnp.where(on, gram, 0.0), keepdims=True)
    factor = lax.rsqrt(trace + 1e-06)
    g = gram * (factor * factor)
    g2 = mm3(g, g)
    eye = jnp.where(on, 1.0, 0.0)
    rest = mm3(g2, 1.6875 * eye - 0.5625 * g + 0.0625 * g2) - 2.4375 * g
    ph, pl_ = split(factor * (2.25 * eye + rest))
    low = mm(jnp.concatenate([top, top], axis=1), jnp.concatenate([ph, pl_], axis=0))
    near_one = jnp.sum(g * g) <= NEAR
    return ph, pl_, low, 2.25 * factor, (factor * rest).astype(bf16), near_one


def final_kernel(got_ref, extra_ref, old_ref, couple_ref, hi_ref, lo_ref, block_hbm, env_hbm, out_hbm, map_ref, env_ref, block_ref, scale_ref, wide_ref, out_ref, sems):
    incoming = pltpu.make_async_copy(block_hbm, block_ref, sems.at[1])
    incoming.start()
    env = two_levels(old_ref, got_ref, couple_ref)
    env_ref[...] = env
    outgoing = pltpu.make_async_copy(env_ref, env_hbm, sems.at[0])
    outgoing.start()
    full_q = got_ref[:, 2 * ROWS : 3 * ROWS].astype(f32).reshape(SIZE, SIZE)
    full_s = got_ref[:, 3 * ROWS :].astype(f32).reshape(SIZE, SIZE)
    ph, pl_, low, scale, rest, near_one = polar_matrices(env, full_q, full_s, extra_ref)
    lh, ll = split(low)
    for k, part in enumerate((ph, ph, pl_, lh, ll, rest)):
        map_ref[k * SIZE : (k + 1) * SIZE] = part
    scale_ref[...] = jnp.broadcast_to(scale, scale_ref.shape)
    incoming.wait()
    step = SIZE // PARTS
    few = step // SENDS

    def taken(ref, i, first_of):
        starts = [b * SIZE + i * step for b in range(first_of, first_of + TOGETHER)]
        return jnp.concatenate([ref[pl.ds(start, step)] for start in starts], axis=0)

    def whole(i, first_of):
        hi, flat = taken(hi_ref, i, first_of), taken(block_ref, i, first_of)
        rows = jnp.concatenate([hi, taken(lo_ref, i, first_of), hi, flat, flat], axis=1)
        return mm(rows, map_ref[: 5 * SIZE])

    def close(i, first_of):
        hi, flat = taken(hi_ref, i, first_of), taken(block_ref, i, first_of)
        value = mm(jnp.concatenate([flat, flat, hi], axis=1), map_ref[3 * SIZE :])
        return value + scale_ref[...] * (hi.astype(f32) + taken(lo_ref, i, first_of).astype(f32))

    def emit(product):
        for i in range(PARTS):
            for first_of in range(0, ROWS, TOGETHER):
                value = product(i, first_of)
                for k in range(TOGETHER):
                    for h in range(2):
                        lines = pl.ds(i * step * ROWS + first_of + k, step, stride=ROWS)
                        wide_ref[h, lines, :] = value[k * step : (k + 1) * step, h * HALF : (h + 1) * HALF]
            for k in range(i * SENDS, (i + 1) * SENDS):
                here = pl.ds(k * few, few)
                for h in range(2):
                    part = wide_ref[h, pl.ds(k * few * ROWS, few * ROWS)].astype(bf16)
                    out_ref[here, :, h * HALF : (h + 1) * HALF] = part.reshape(few, ROWS, HALF)
                copy(k).start()

    def copy(k):
        here = pl.ds(k * few, few)
        return pltpu.make_async_copy(out_ref.at[here], out_hbm.at[here], sems.at[2 + k])

    pl.when(near_one)(lambda: emit(close))
    pl.when(jnp.logical_not(near_one))(lambda: emit(whole))
    for k in range(PARTS * SENDS):
        copy(k).wait()
    outgoing.wait()


def exchange(x, axis, groups=None):
    return lax.all_to_all(x, axis, 0, 0, axis_index_groups=groups, tiled=True)


def permuted(x, axis, route):
    return lax.ppermute(x, axis, [(i, route(i)) for i in range(lax.axis_size(axis))])


square = ((SIZE, SIZE), f32)
kept = pltpu.HBM((SIZE, SIZE), f32)
sliced = ((4, ROWS, SIZE), f32)


def ascend(iso, left, right):
    return call(
        ascend_kernel,
        "ascend",
        [((WIDTH, 2, ROWS, SIZE), f32)],
        scratch=[
            pltpu.VMEM((SIZE, ROWS, SIZE), bf16),
            pltpu.VMEM((2 * SIZE, SIZE), bf16),
            pltpu.VMEM((2, FLAT, HALF), f32),
            pltpu.VMEM((SIZE, FLAT), bf16),
            pltpu.VMEM((2, FLAT, 2 * SIZE), bf16),
            pltpu.SemaphoreType.DMA((CHUNKS + 2,)),
        ],
        in_specs=[pl.BlockSpec(memory_space=pl.ANY)] * 3,
        out_specs=[pl.BlockSpec(memory_space=pltpu.VMEM)],
        grant=24,
        flops=6 << 29,
    )(in_hbm(iso), in_hbm(left), in_hbm(right))[0]


def prepare(iso, after):
    return call(
        prepare_kernel,
        "prepare",
        [pltpu.HBM((FLAT, SIZE), bf16), pltpu.HBM((SIZE, FLAT), bf16), square],
        scratch=[
            pltpu.VMEM((2, FLAT, HALF), f32),
            pltpu.VMEM((FLAT, SIZE), bf16),
            pltpu.VMEM((SIZE, FLAT), bf16),
            pltpu.SemaphoreType.DMA((2,)),
        ],
        in_specs=[pl.BlockSpec(memory_space=pltpu.VMEM), pl.BlockSpec(memory_space=pl.ANY)],
        out_specs=[pl.BlockSpec(memory_space=pl.ANY)] * 2 + [pl.BlockSpec(memory_space=pltpu.VMEM)],
        flops=1 << 29,
    )(iso, after)


def rounded(got, *after):
    return call(round_kernel, "rounded", [((WIDTH, 2, ROWS, SIZE), bf16)], ins=3, unread=2)(got, *after)[0]


def first(index, own, near, couple, foreign):
    return call(first_kernel, "first", [kept, sliced], ins=5, smem=1)(
        index, own, near, couple, foreign
    )


def gradient(index, block, turned, edge, near, far, norm, after):
    vmem = pl.BlockSpec(memory_space=pltpu.VMEM)
    any_place = pl.BlockSpec(memory_space=pl.ANY)
    return call(
        gradient_kernel,
        "gradient",
        [pltpu.HBM((FLAT, SIZE), bf16), pltpu.HBM((FLAT, SIZE), bf16), ((WIDTH, 2 * ROWS + EXTRA, SIZE), bf16)],
        scratch=[
            pltpu.VMEM((FLAT, SIZE), bf16),
            pltpu.VMEM((FLAT, SIZE), bf16),
            pltpu.VMEM((SIZE, FLAT), bf16),
            pltpu.VMEM((FLAT, SIZE), bf16),
            pltpu.VMEM((SIZE, FLAT), bf16),
            pltpu.SemaphoreType.DMA((4 * CHUNKS,)),
        ],
        in_specs=[pl.BlockSpec(memory_space=pltpu.SMEM)] + [vmem] * 4 + [any_place] * 3,
        out_specs=[any_place] * 2 + [vmem],
        flops=4 << 29,
        grant=20,
    )(index, in_hbm(edge), in_hbm(near), far, norm, in_hbm(block), in_hbm(turned), after)


def pack(got, parts, foreign):
    return call(pack_kernel, "pack", [((WIDTH, 6 * ROWS + EXTRA, SIZE), bf16)], ins=3)(got, parts, foreign)[0]


def repeat(got, sums):
    return call(repeat_kernel, "repeat", [((WIDTH, 4 * ROWS, SIZE), bf16)], ins=2)(got, sums)[0]


def second(index, got, old, couple):
    return call(
        second_kernel,
        "second",
        [square, sliced, ((2 * ROWS, SIZE), bf16), ((EXTRA, SIZE), f32)],
        ins=4,
        smem=1,
    )(index, got, in_hbm(old), couple)


def final(got, extra, old, couple, hi, lo, block):
    vmem = pl.BlockSpec(memory_space=pltpu.VMEM)
    any_place = pl.BlockSpec(memory_space=pl.ANY)
    return call(
        final_kernel,
        "final",
        [pltpu.HBM((SIZE, SIZE), f32), pltpu.HBM((SIZE, ROWS, SIZE), bf16)],
        scratch=[
            pltpu.VMEM((6 * SIZE, SIZE), bf16),
            pltpu.VMEM((SIZE, SIZE), f32),
            pltpu.VMEM((FLAT, SIZE), bf16),
            pltpu.VMEM((1, SIZE), f32),
            pltpu.VMEM((2, FLAT, HALF), f32),
            pltpu.VMEM((SIZE, ROWS, SIZE), bf16),
            pltpu.SemaphoreType.DMA((2 + PARTS * SENDS,)),
        ],
        in_specs=[vmem] * 6 + [any_place],
        out_specs=[any_place] * 2,
        flops=5 << 29,
        grant=20,
    )(got, extra, old, couple, hi, lo, in_hbm(block))


def body(iso, edge_left, edge_right, coupling):
    iso, left, right, couple = iso[0], edge_left[0], edge_right[0], coupling[0]
    s = lax.axis_index("blk")
    j = lax.axis_index("bond")
    z = s // 2
    index = jnp.stack([j, z % 4, s % 2, z // 4]).astype(jnp.int32)

    couple_1 = permuted(couple, "blk", lambda i: i ^ 2)
    part_2 = lax.dynamic_slice_in_dim(couple, j * ROWS, ROWS, 0)
    part_2 = permuted(part_2, "blk", lambda i: i ^ 8)

    blocks = ascend(iso, left, right)
    block, turned, norm = prepare(iso, blocks)
    share = rounded(exchange(blocks, "bond"), norm, part_2)
    own = exchange(share, "bond")
    near = permuted(own, "blk", lambda i: i ^ 1)
    far = permuted(own, "blk", lambda i: (i + 1) % 32 if i % 2 else (i - 1) % 32)

    quads = [[(zq * 4 + zl) * 2 + c for zl in range(4)] for zq in range(4) for c in range(2)]
    strides = [[(zh * 4 + zl) * 2 + c for zh in range(4)] for zl in range(4) for c in range(2)]

    env, outgoing = first(index, own, near, couple, couple_1)
    incoming = exchange(outgoing, "blk", quads)
    moved_hi, moved_lo, parts = gradient(index, block, turned, left, near, far, norm, outgoing)
    got = exchange(pack(incoming, parts, part_2), "bond")
    env, outgoing, sums, extra = second(index, got, env, couple)
    incoming = exchange(outgoing, "blk", strides)
    got = exchange(repeat(incoming, sums), "bond")
    env, out = final(got, extra, env, couple, moved_hi, moved_lo, block)
    return (out[None], env[None])


def solution(mesh):
    placed = (
        P("blk", None, "bond", None),
        P("blk", None, None),
        P("blk", None, None),
        P("blk", None, None),
    )
    return jax.shard_map(
        body,
        mesh=mesh,
        in_specs=placed,
        out_specs=(P("blk", None, "bond", None), P("blk", None, None)),
        check_vma=False,
    )
```

```python
import jax
import jax.numpy as jnp
from jax import lax
from jax.experimental import pallas as pl
from jax.experimental.pallas import tpu as pltpu
from jax.sharding import PartitionSpec as P

bf16 = jnp.bfloat16
f32 = jnp.float32
NN = ((1,), (0,))
NT = ((1,), (1,))
SIZE = 256
WIDTH = 16
ROWS = SIZE // WIDTH
FLAT = SIZE * ROWS
HALF = 128
CHUNKS = 4
EXTRA = 16
PARTS = 2
TOGETHER = 8
SENDS = 4
NEAR = 0.01


def split(x):
    hi = x.astype(bf16)
    return hi, (x - hi.astype(f32)).astype(bf16)


def mm(a, b, dims=NN):
    return lax.dot_general(a, b, (dims, ((), ())), preferred_element_type=f32)


def mm3(a, b, dims=NN):
    ah, al = split(a)
    bh, bl = split(b)
    rows = jnp.concatenate([ah, ah, al], axis=1)
    return mm(rows, jnp.concatenate([bh, bl, bh], axis=dims[1][0]), dims)


def sandwich(c, e):
    return mm3(mm3(c, e), c, NT)


def in_hbm(x):
    return pltpu.with_memory_space_constraint(x, pltpu.HBM)


def iotas():
    shape = (SIZE, SIZE)
    return lax.broadcasted_iota(jnp.int32, shape, 0), lax.broadcasted_iota(jnp.int32, shape, 1)


def call(kernel, name, outs, scratch=(), smem=0, unread=0, ins=0, flops=0, grant=16, grid=None, in_specs=None, out_specs=None):
    vmem = pl.BlockSpec(memory_space=pltpu.VMEM)
    any_place = pl.BlockSpec(memory_space=pl.ANY)
    if in_specs is None:
        in_specs = (
            [pl.BlockSpec(memory_space=pltpu.SMEM)] * smem
            + [vmem] * (ins - smem - unread)
            + [any_place] * unread
        )
        out_specs = [vmem] * len(outs)
    params = dict(grid=grid) if grid else {}
    return pl.pallas_call(
        kernel,
        name=name,
        out_shape=[o if isinstance(o, pl.MemoryRef) else jax.ShapeDtypeStruct(*o) for o in outs],
        in_specs=in_specs,
        out_specs=out_specs,
        scratch_shapes=scratch,
        compiler_params=pltpu.CompilerParams(vmem_limit_bytes=grant << 20),
        cost_estimate=pl.CostEstimate(flops=flops, bytes_accessed=4 << 20, transcendentals=0),
        **params,
    )


def spread_rows(iso_ref, wide_ref):
    wide = iso_ref[...].reshape(FLAT, SIZE).astype(f32)
    wide_ref[0] = wide[:, :HALF]
    wide_ref[1] = wide[:, HALF:]


def bond_slice(wide_ref, b):
    rows = pl.ds(b, SIZE, stride=ROWS)
    return jnp.concatenate([wide_ref[h, rows, :].astype(bf16) for h in range(2)], axis=1)


def ascend_kernel(iso_hbm, left_hbm, right_hbm, out_ref, iso_ref, edge_ref, wide_ref, turned_ref, mapped_ref, sems):
    step = SIZE // CHUNKS
    copies = []
    for i in range(CHUNKS):
        here = pl.ds(i * step, step)
        copies.append(pltpu.make_async_copy(iso_hbm.at[here], iso_ref.at[here], sems.at[i]))
    edge_copies = [
        pltpu.make_async_copy(left_hbm, edge_ref.at[pl.ds(0, SIZE)], sems.at[CHUNKS]),
        pltpu.make_async_copy(right_hbm, edge_ref.at[pl.ds(SIZE, SIZE)], sems.at[CHUNKS + 1]),
    ]
    for copy in copies + edge_copies:
        copy.start()
    for i, copy in enumerate(copies):
        copy.wait()
        wide = iso_ref[i * step : (i + 1) * step].reshape(step * ROWS, SIZE).astype(f32)
        for h in range(2):
            wide_ref[h, i * step * ROWS : (i + 1) * step * ROWS] = wide[:, h * HALF : (h + 1) * HALF]
    for copy in edge_copies:
        copy.wait()
    edges = edge_ref[...]
    total = jnp.zeros((SIZE, 2 * SIZE), f32)
    for b in range(ROWS + 2):
        if b < ROWS:
            block = bond_slice(wide_ref, b)
            here = slice(b * SIZE, (b + 1) * SIZE)
            turned_ref[:, here] = block.T
            for k, part in enumerate(split(mm(edges, block))):
                mapped_ref[k, here, :SIZE] = part[:SIZE]
                mapped_ref[k, here, SIZE:] = part[SIZE:]
        if b >= 2 and b % 2 == 1:
            past = slice((b - 3) * SIZE, (b - 1) * SIZE)
            turned = turned_ref[:, past]
            total = total + (mm(turned, mapped_ref[0, past]) + mm(turned, mapped_ref[1, past]))
    for k in range(2):
        out_ref[:, k] = total[:, k * SIZE : (k + 1) * SIZE].reshape(WIDTH, ROWS, SIZE)


def prepare_kernel(iso_ref, after_ref, block_hbm, turned_hbm, norm_ref, wide_ref, block_ref, turned_ref, sems):
    spread_rows(iso_ref, wide_ref)
    for b in range(ROWS):
        block = bond_slice(wide_ref, b)
        here = slice(b * SIZE, (b + 1) * SIZE)
        block_ref[here] = block
        turned_ref[:, here] = block.T
    copies = [
        pltpu.make_async_copy(block_ref, block_hbm, sems.at[0]),
        pltpu.make_async_copy(turned_ref, turned_hbm, sems.at[1]),
    ]
    for copy in copies:
        copy.start()
    norm_ref[...] = mm(turned_ref[...], block_ref[...])
    for copy in copies:
        copy.wait()


def round_kernel(got_ref, after_ref, also_ref, out_ref):
    share = got_ref[0]
    for i in range(1, WIDTH):
        share = share + got_ref[i]
    share = share.astype(bf16)
    for i in range(WIDTH):
        out_ref[i] = share


def slices(index_ref, place, env_ref, left, foreign, out_ref):
    own = env_ref[pl.ds(index_ref[0] * ROWS, ROWS), :]
    crossed = mm3(mm3(left, env_ref[...]), foreign, NT)
    for p in range(4):
        which = index_ref[place] ^ p
        out_ref[p] = jnp.where(which == 3, crossed, jnp.where(which == 0, 0.0, own))


def first_kernel(index_ref, own_ref, near_ref, couple_ref, foreign_ref, env_ref, out_ref):
    def whole(ref):
        return (ref[:, 0].astype(f32) + ref[:, 1].astype(f32)).reshape(SIZE, SIZE)

    env_ref[...] = 0.5 * (whole(own_ref) + sandwich(couple_ref[...], whole(near_ref)))
    left = foreign_ref[pl.ds(index_ref[0] * ROWS, ROWS), :]
    slices(index_ref, 1, env_ref, left, foreign_ref[...], out_ref)


def gradient_kernel(index_ref, edge_ref, near_ref, far_ref, norm_ref, block_hbm, turned_hbm, after_ref, hi_hbm, lo_hbm, out_ref, moved_ref, low_ref, flipped_ref, block_ref, turned_ref, sems):
    copies = []
    step = FLAT // CHUNKS
    for i in range(CHUNKS):
        here = pl.ds(i * step, step)
        copies.append(pltpu.make_async_copy(block_hbm.at[here], block_ref.at[here], sems.at[2 * i]))
        copies.append(pltpu.make_async_copy(turned_hbm.at[:, here], turned_ref.at[:, here], sems.at[2 * i + 1]))
    for copy in copies:
        copy.start()
    odd = index_ref[2] == 1

    def whole(ref, k):
        return ref[:, k].astype(f32).reshape(SIZE, SIZE)

    from_left = jnp.where(odd, whole(near_ref, 1), whole(far_ref, 1))
    from_right = jnp.where(odd, whole(far_ref, 0), whole(near_ref, 0))
    mix = (edge_ref[...].astype(f32) + from_left + from_right).astype(bf16)
    squares = jnp.zeros((8, SIZE), f32)
    outgoing = []
    for b in range(ROWS):
        i, first_of = divmod(b, ROWS // CHUNKS)
        if first_of == 0:
            copies[2 * i].wait()
            copies[2 * i + 1].wait()
        here = slice(b * SIZE, (b + 1) * SIZE)
        moved = mm(mix, block_ref[here])
        squares = squares + jnp.sum((moved * moved).reshape(SIZE // 8, 8, SIZE), axis=0)
        moved_ref[here], low_ref[here] = split(moved)
        flipped_ref[:, here] = mm(turned_ref[:, here], mix, NT).astype(bf16)
        if first_of == ROWS // CHUNKS - 1:
            here = pl.ds(i * step, step)
            for k, (ref, hbm) in enumerate(((moved_ref, hi_hbm), (low_ref, lo_hbm))):
                copy = pltpu.make_async_copy(ref.at[here], hbm.at[here], sems.at[2 * (CHUNKS + i) + k])
                copy.start()
                outgoing.append(copy)
    part_q = mm(turned_ref[...], moved_ref[...])
    part_r = mm(flipped_ref[...], moved_ref[...])
    part_n = norm_ref[...]
    row, col = iotas()
    diag_n = jnp.sum(jnp.where(row == col, part_n, 0.0), axis=0, keepdims=True)
    diag_r = jnp.sum(squares, axis=0, keepdims=True)
    part_r = jnp.where(row == col, diag_r, part_r)
    nh, nl = split(diag_n)
    _, rl = split(diag_r)
    extra = jnp.concatenate(
        [nh.astype(f32), nl.astype(f32), rl.astype(f32), jnp.zeros((EXTRA - 3, SIZE), f32)], axis=0
    ).astype(bf16)
    packed = jnp.where(row < col, part_n, part_r)
    out_ref[:, :ROWS] = part_q.astype(bf16).reshape(WIDTH, ROWS, SIZE)
    out_ref[:, ROWS : 2 * ROWS] = packed.astype(bf16).reshape(WIDTH, ROWS, SIZE)
    for i in range(WIDTH):
        out_ref[i, 2 * ROWS :] = extra
    for copy in outgoing:
        copy.wait()


def pack_kernel(got_ref, parts_ref, foreign_ref, out_ref):
    hi, lo = split((got_ref[0] + got_ref[1]) + (got_ref[2] + got_ref[3]))
    foreign_hi, foreign_lo = split(foreign_ref[...])
    for i in range(WIDTH):
        out_ref[i, :ROWS] = hi
        out_ref[i, ROWS : 2 * ROWS] = lo
        out_ref[i, 4 * ROWS : 5 * ROWS] = foreign_hi
        out_ref[i, 5 * ROWS : 6 * ROWS] = foreign_lo
    out_ref[:, 2 * ROWS : 4 * ROWS] = parts_ref[:, : 2 * ROWS]
    out_ref[:, 6 * ROWS :] = parts_ref[:, 2 * ROWS :]


def repeat_kernel(got_ref, sums_ref, out_ref):
    hi, lo = split((got_ref[0] + got_ref[1]) + (got_ref[2] + got_ref[3]))
    for i in range(WIDTH):
        out_ref[i, :ROWS] = hi
        out_ref[i, ROWS : 2 * ROWS] = lo
        out_ref[i, 2 * ROWS :] = sums_ref[...]


def two_levels(env_ref, got_ref, couple_ref):
    force = got_ref[:, :ROWS].astype(f32) + got_ref[:, ROWS : 2 * ROWS].astype(f32)
    return 0.25 * (env_ref[...] + sandwich(couple_ref[...], force.reshape(SIZE, SIZE)))


def second_kernel(index_ref, got_ref, old_ref, couple_ref, env_ref, out_ref, sums_ref, extra_ref):
    env_ref[...] = two_levels(old_ref, got_ref, couple_ref)

    def foreign(at):
        hi, lo = slice(4 * ROWS, 5 * ROWS), slice(5 * ROWS, 6 * ROWS)
        return got_ref[at, hi].astype(f32) + got_ref[at, lo].astype(f32)

    left = foreign(index_ref[0])
    slices(index_ref, 3, env_ref, left, foreign(slice(None)).reshape(SIZE, SIZE), out_ref)

    def total(rows):
        value = got_ref[0, rows].astype(f32)
        for i in range(1, WIDTH):
            value = value + got_ref[i, rows].astype(f32)
        return value

    extra_ref[...] = total(slice(6 * ROWS, 6 * ROWS + EXTRA))
    sums_ref[...] = total(slice(2 * ROWS, 4 * ROWS)).astype(bf16)


def mm2(a, b, dims=NN):
    ah, al = split(a)
    return mm(jnp.concatenate([ah, al], axis=1), jnp.concatenate([b, b], axis=0), dims)


def polar_matrices(env, full_q, full_s, extra_ref):
    row, col = iotas()
    on = row == col
    top = env.astype(bf16)
    lower = jnp.where(row > col, full_s, 0.0)
    upper = jnp.where(row < col, full_s, 0.0)
    full_n = upper + upper.T + jnp.where(on, extra_ref[0:1, :] + extra_ref[1:2, :], 0.0)
    full_r = lower + lower.T + jnp.where(on, full_s + extra_ref[2:3, :], 0.0)
    half = full_q + 0.5 * mm2(full_n, top)
    hh, hl = split(half)
    turned = top.T
    side = mm(jnp.concatenate([turned, turned], axis=1), jnp.concatenate([hh, hl], axis=0))
    gram = full_r + side + side.T
    trace = jnp.sum(jnp.where(on, gram, 0.0), keepdims=True)
    factor = lax.rsqrt(trace + 1e-06)
    g = gram * (factor * factor)
    g2 = mm3(g, g)
    eye = jnp.where(on, 1.0, 0.0)
    rest = mm3(g2, 1.6875 * eye - 0.5625 * g + 0.0625 * g2) - 2.4375 * g
    ph, pl_ = split(factor * (2.25 * eye + rest))
    low = mm(jnp.concatenate([top, top], axis=1), jnp.concatenate([ph, pl_], axis=0))
    near_one = jnp.sum(g * g) <= NEAR
    return ph, pl_, low, 2.25 * factor, (factor * rest).astype(bf16), near_one


def final_kernel(got_ref, extra_ref, old_ref, couple_ref, hi_ref, lo_ref, block_hbm, env_hbm, out_hbm, map_ref, env_ref, block_ref, scale_ref, wide_ref, out_ref, sems):
    incoming = pltpu.make_async_copy(block_hbm, block_ref, sems.at[1])
    incoming.start()
    env = two_levels(old_ref, got_ref, couple_ref)
    env_ref[...] = env
    outgoing = pltpu.make_async_copy(env_ref, env_hbm, sems.at[0])
    outgoing.start()
    full_q = got_ref[:, 2 * ROWS : 3 * ROWS].astype(f32).reshape(SIZE, SIZE)
    full_s = got_ref[:, 3 * ROWS :].astype(f32).reshape(SIZE, SIZE)
    ph, pl_, low, scale, rest, near_one = polar_matrices(env, full_q, full_s, extra_ref)
    lh, ll = split(low)
    for k, part in enumerate((ph, ph, pl_, lh, ll, rest)):
        map_ref[k * SIZE : (k + 1) * SIZE] = part
    scale_ref[...] = jnp.broadcast_to(scale, scale_ref.shape)
    incoming.wait()
    step = SIZE // PARTS
    few = step // SENDS

    def taken(ref, i, first_of):
        starts = [b * SIZE + i * step for b in range(first_of, first_of + TOGETHER)]
        return jnp.concatenate([ref[pl.ds(start, step)] for start in starts], axis=0)

    def whole(i, first_of):
        hi, flat = taken(hi_ref, i, first_of), taken(block_ref, i, first_of)
        rows = jnp.concatenate([hi, taken(lo_ref, i, first_of), hi, flat, flat], axis=1)
        return mm(rows, map_ref[: 5 * SIZE])

    def close(i, first_of):
        hi, flat = taken(hi_ref, i, first_of), taken(block_ref, i, first_of)
        value = mm(jnp.concatenate([flat, flat, hi], axis=1), map_ref[3 * SIZE :])
        return value + scale_ref[...] * (hi.astype(f32) + taken(lo_ref, i, first_of).astype(f32))

    def emit(product):
        for i in range(PARTS):
            for first_of in range(0, ROWS, TOGETHER):
                value = product(i, first_of)
                for k in range(TOGETHER):
                    for h in range(2):
                        lines = pl.ds(i * step * ROWS + first_of + k, step, stride=ROWS)
                        wide_ref[h, lines, :] = value[k * step : (k + 1) * step, h * HALF : (h + 1) * HALF]
            for k in range(i * SENDS, (i + 1) * SENDS):
                here = pl.ds(k * few, few)
                for h in range(2):
                    part = wide_ref[h, pl.ds(k * few * ROWS, few * ROWS)].astype(bf16)
                    out_ref[here, :, h * HALF : (h + 1) * HALF] = part.reshape(few, ROWS, HALF)
                copy(k).start()

    def copy(k):
        here = pl.ds(k * few, few)
        return pltpu.make_async_copy(out_ref.at[here], out_hbm.at[here], sems.at[2 + k])

    pl.when(near_one)(lambda: emit(close))
    pl.when(jnp.logical_not(near_one))(lambda: emit(whole))
    for k in range(PARTS * SENDS):
        copy(k).wait()
    outgoing.wait()


def exchange(x, axis, groups=None):
    return lax.all_to_all(x, axis, 0, 0, axis_index_groups=groups, tiled=True)


def permuted(x, axis, route):
    return lax.ppermute(x, axis, [(i, route(i)) for i in range(lax.axis_size(axis))])


square = ((SIZE, SIZE), f32)
kept = pltpu.HBM((SIZE, SIZE), f32)
sliced = ((4, ROWS, SIZE), f32)


def ascend(iso, left, right):
    return call(
        ascend_kernel,
        "ascend",
        [((WIDTH, 2, ROWS, SIZE), f32)],
        scratch=[
            pltpu.VMEM((SIZE, ROWS, SIZE), bf16),
            pltpu.VMEM((2 * SIZE, SIZE), bf16),
            pltpu.VMEM((2, FLAT, HALF), f32),
            pltpu.VMEM((SIZE, FLAT), bf16),
            pltpu.VMEM((2, FLAT, 2 * SIZE), bf16),
            pltpu.SemaphoreType.DMA((CHUNKS + 2,)),
        ],
        in_specs=[pl.BlockSpec(memory_space=pl.ANY)] * 3,
        out_specs=[pl.BlockSpec(memory_space=pltpu.VMEM)],
        grant=24,
        flops=6 << 29,
    )(in_hbm(iso), in_hbm(left), in_hbm(right))[0]


def prepare(iso, after):
    return call(
        prepare_kernel,
        "prepare",
        [pltpu.HBM((FLAT, SIZE), bf16), pltpu.HBM((SIZE, FLAT), bf16), square],
        scratch=[
            pltpu.VMEM((2, FLAT, HALF), f32),
            pltpu.VMEM((FLAT, SIZE), bf16),
            pltpu.VMEM((SIZE, FLAT), bf16),
            pltpu.SemaphoreType.DMA((2,)),
        ],
        in_specs=[pl.BlockSpec(memory_space=pltpu.VMEM), pl.BlockSpec(memory_space=pl.ANY)],
        out_specs=[pl.BlockSpec(memory_space=pl.ANY)] * 2 + [pl.BlockSpec(memory_space=pltpu.VMEM)],
        flops=1 << 29,
    )(iso, after)


def rounded(got, *after):
    return call(round_kernel, "rounded", [((WIDTH, 2, ROWS, SIZE), bf16)], ins=3, unread=2)(got, *after)[0]


def first(index, own, near, couple, foreign):
    return call(first_kernel, "first", [kept, sliced], ins=5, smem=1)(
        index, own, near, couple, foreign
    )


def gradient(index, block, turned, edge, near, far, norm, after):
    vmem = pl.BlockSpec(memory_space=pltpu.VMEM)
    any_place = pl.BlockSpec(memory_space=pl.ANY)
    return call(
        gradient_kernel,
        "gradient",
        [pltpu.HBM((FLAT, SIZE), bf16), pltpu.HBM((FLAT, SIZE), bf16), ((WIDTH, 2 * ROWS + EXTRA, SIZE), bf16)],
        scratch=[
            pltpu.VMEM((FLAT, SIZE), bf16),
            pltpu.VMEM((FLAT, SIZE), bf16),
            pltpu.VMEM((SIZE, FLAT), bf16),
            pltpu.VMEM((FLAT, SIZE), bf16),
            pltpu.VMEM((SIZE, FLAT), bf16),
            pltpu.SemaphoreType.DMA((4 * CHUNKS,)),
        ],
        in_specs=[pl.BlockSpec(memory_space=pltpu.SMEM)] + [vmem] * 4 + [any_place] * 3,
        out_specs=[any_place] * 2 + [vmem],
        flops=4 << 29,
        grant=20,
    )(index, in_hbm(edge), in_hbm(near), far, norm, in_hbm(block), in_hbm(turned), after)


def pack(got, parts, foreign):
    return call(pack_kernel, "pack", [((WIDTH, 6 * ROWS + EXTRA, SIZE), bf16)], ins=3)(got, parts, foreign)[0]


def repeat(got, sums):
    return call(repeat_kernel, "repeat", [((WIDTH, 4 * ROWS, SIZE), bf16)], ins=2)(got, sums)[0]


def second(index, got, old, couple):
    return call(
        second_kernel,
        "second",
        [square, sliced, ((2 * ROWS, SIZE), bf16), ((EXTRA, SIZE), f32)],
        ins=4,
        smem=1,
    )(index, got, in_hbm(old), couple)


def final(got, extra, old, couple, hi, lo, block):
    vmem = pl.BlockSpec(memory_space=pltpu.VMEM)
    any_place = pl.BlockSpec(memory_space=pl.ANY)
    return call(
        final_kernel,
        "final",
        [pltpu.HBM((SIZE, SIZE), f32), pltpu.HBM((SIZE, ROWS, SIZE), bf16)],
        scratch=[
            pltpu.VMEM((6 * SIZE, SIZE), bf16),
            pltpu.VMEM((SIZE, SIZE), f32),
            pltpu.VMEM((FLAT, SIZE), bf16),
            pltpu.VMEM((1, SIZE), f32),
            pltpu.VMEM((2, FLAT, HALF), f32),
            pltpu.VMEM((SIZE, ROWS, SIZE), bf16),
            pltpu.SemaphoreType.DMA((2 + PARTS * SENDS,)),
        ],
        in_specs=[vmem] * 6 + [any_place],
        out_specs=[any_place] * 2,
        flops=5 << 29,
        grant=20,
    )(got, extra, old, couple, hi, lo, in_hbm(block))


def body(iso, edge_left, edge_right, coupling):
    iso, left, right, couple = iso[0], edge_left[0], edge_right[0], coupling[0]
    s = lax.axis_index("blk")
    j = lax.axis_index("bond")
    z = s // 2
    index = jnp.stack([j, z % 4, s % 2, z // 4]).astype(jnp.int32)

    couple_1 = permuted(couple, "blk", lambda i: i ^ 2)
    part_2 = lax.dynamic_slice_in_dim(couple, j * ROWS, ROWS, 0)
    part_2 = permuted(part_2, "blk", lambda i: i ^ 8)

    blocks = ascend(iso, left, right)
    block, turned, norm = prepare(iso, blocks)
    share = rounded(exchange(blocks, "bond"), norm, part_2)
    own = exchange(share, "bond")
    near = permuted(own, "blk", lambda i: i ^ 1)
    far = permuted(own, "blk", lambda i: (i + 1) % 32 if i % 2 else (i - 1) % 32)

    quads = [[(zq * 4 + zl) * 2 + c for zl in range(4)] for zq in range(4) for c in range(2)]
    strides = [[(zh * 4 + zl) * 2 + c for zh in range(4)] for zl in range(4) for c in range(2)]

    env, outgoing = first(index, own, near, couple, couple_1)
    incoming = exchange(outgoing, "blk", quads)
    moved_hi, moved_lo, parts = gradient(index, block, turned, left, near, far, norm, outgoing)
    got = exchange(pack(incoming, parts, part_2), "bond")
    env, outgoing, sums, extra = second(index, got, env, couple)
    incoming = exchange(outgoing, "blk", strides)
    got = exchange(repeat(incoming, sums), "bond")
    env, out = final(got, extra, env, couple, moved_hi, moved_lo, block)
    return (out[None], env[None])


def solution(mesh):
    placed = (
        P("blk", None, "bond", None),
        P("blk", None, None),
        P("blk", None, None),
        P("blk", None, None),
    )
    return jax.shard_map(
        body,
        mesh=mesh,
        in_specs=placed,
        out_specs=(P("blk", None, "bond", None), P("blk", None, None)),
        check_vma=False,
    )
```
